256 devices in a mesh: tiles: 64 (over y, x_hi, z), lev: 4 (over x_lo, core).
Axes of the slice: x: 4 (x_hi: 2, x_lo: 2; x = x_hi * 2 + x_lo), y: 4, z: 8, core: 2. Of those that a mesh axis runs over, the one named last changes fastest.
Arguments:
- air_state: float32 [4, 8, 1048576], P(None, 'lev', 'tiles'), may hold values from -6 to 6
- sea_state: float32 [4, 8, 1048576], P(None, 'lev', 'tiles'), may hold values from -6 to 6
- air_courant: float32 [8, 1048576], P('lev', 'tiles'), may hold values from -0.9 to 0.9
- sea_courant: float32 [8, 1048576], P('lev', 'tiles'), may hold values from -0.9 to 0.9
- air_mixing: float32 [8, 1048576], P(None, 'tiles'), may hold values from 0.2 to 3
- sea_mixing: float32 [8, 1048576], P(None, 'tiles'), may hold values from 0.2 to 3
- upward_weight: bfloat16 [16384, 2, 4096], P('tiles'), may hold values from 0 to 0.03125
- upward_target: int32 [16384, 2], P('tiles'), may hold values from 0 to 63, all different within a row; in each aligned block of 256 rows (0 to 255, 256 to 511, ...) at most 16 rows name the same one
- upward_block: int32 [16384, 2], P('tiles'), may hold values from 0 to 255
- downward_weight: bfloat16 [16384, 2, 4096], P('tiles'), may hold values from 0 to 0.03125
- downward_target: int32 [16384, 2], P('tiles'), may hold values from 0 to 63, all different within a row; in each aligned block of 256 rows (0 to 255, 256 to 511, ...) at most 16 rows name the same one
- downward_block: int32 [16384, 2], P('tiles'), may hold values from 0 to 255
- sea_mask: int32 [16384], P('tiles'), may hold values 0 or 1
Outputs:
- air_out: float32 [4, 8, 1048576], P('lev', None, 'tiles')
- sea_out: float32 [4, 8, 1048576], P('lev', None, 'tiles')
The draws below stay inside these ranges and needn't reach their ends.
Inputs may be any that keep to these rules, and one draw needn't show every extreme that they name: `upward_target`: each row names 2 different tiles indices; among the 256 rows of one tiles index no tiles index is named more than 16 times, a bound that some block reaches. `downward_target`: each row names 2 different tiles indices; among the 256 rows of one tiles index no tiles index is named more than 16 times, a bound that some block reaches.
All inputs are finite; a program needn't handle non-finite values. No bound on the sum of `sea_mask` on one device may be relied on, other than what follows from the above.
Results may differ from the reference program's by a relative error of at most 0.0003.
Values sent between devices are 32-bit elements; how exact they have to be, the bound alone decides.
No kernel may reach another device: no remote copies, remote signals or barrier semaphores. Data moves between devices by JAX's collectives and lax.ppermute only.
A program may use at most 128 MiB of HBM per device.

```python
import math
import jax
import jax.numpy as jnp
import numpy as np
from jax import lax

LEV = 8
NVAR = 4
BLOCK = 64
MAP_K = 2
ASTEPS = 2
BLK_DEV = 256
NCELL = 1048576
NBLK = 16384
CAP = 16
N_TILES = 64


def plant(entries, stream_key, low, top_value):
    extent = entries.shape
    spot = [jax.random.randint(jax.random.fold_in(stream_key, axis), (), 0, extent[axis]) for axis in range(len(extent))]
    entries = entries.at[tuple(spot)].set(low)
    longest = extent.index(max(extent))
    spot[longest] = (spot[longest] + 1) % extent[longest]
    return entries.at[tuple(spot)].set(top_value)


def shard_levels(own_key, extent, shards, low, high):
    factor_of, own = 1.0, jax.random.fold_in(own_key, 6)
    for axis_at, blocks in shards:
        heights = jnp.exp(jax.random.uniform(jax.random.fold_in(own, axis_at), (blocks,), jnp.float32, low / len(shards), high / len(shards)))
        factor_of = factor_of * jnp.repeat(heights, extent[axis_at] // blocks).reshape([-1 if axis == axis_at else 1 for axis in range(len(extent))])
    return factor_of


def shared_out(own_key, own, number, rows, number_of, top, bound, skew):
    order = jax.random.permutation(own_key, number_of)
    heavy_load, common = load_shares(number_of, rows * top, bound, skew, True), load_shares(number_of, rows * top, bound, skew, False)
    places = jnp.arange(number_of)

    def named(sizes, offset_by):
        used = int((sizes > 0).sum())
        fixed = max(1, used // 4)
        shifted = fixed + (places - fixed + offset_by * (used - fixed)) % max(1, number_of - fixed)
        return jnp.zeros((number_of,), jnp.int32).at[order[jnp.where(places < fixed, places, shifted)]].set(jnp.asarray(sizes, jnp.int32))

    sizes = jnp.where(number % 4 == 0, named(heavy_load, number // 4), named(common, number - number // 4 - 1))
    mixed = jax.random.permutation(jax.random.fold_in(own, 3), number_of)
    donor, taker = mixed[0:number_of // 2 * 2:2], mixed[1:number_of // 2 * 2:2]
    room = jnp.minimum(sizes[donor] - 1, bound - sizes[taker]) // 2
    room = jnp.where((donor == order[0]) | (taker == order[0]) | (sizes[taker] == 0), 0, jnp.maximum(room, 0))
    shifted = jax.random.randint(jax.random.fold_in(own, 4), (number_of // 2,), 0, 1 << 20) % (room + 1)
    sizes = sizes.at[donor].add(-shifted).at[taker].add(shifted)
    labels = jnp.searchsorted(jnp.cumsum(sizes), jnp.arange(rows * top), side="right").astype(jnp.int32)
    grid = labels.reshape(top, rows).T
    grid = grid[jax.random.permutation(jax.random.fold_in(own, 1), rows)]
    offset_by = jax.random.randint(jax.random.fold_in(own, 2), (rows, 1), 0, top)
    return jnp.take_along_axis(grid, (jnp.arange(top)[None, :] + offset_by) % top, axis=1)


def load_shares(count, total, reach, skew, full):
    weights = [(1 << 20) // math.isqrt(rank ** skew) + 1 for rank in range(1, count + 1)]
    largest = reach if full else min(reach, max(-(-total // count), total * weights[0] // sum(weights)))
    least = 1 if total - largest >= count - 1 else 0
    holding, rest = [largest] + [least] * (count - 1), total - largest - least * (count - 1)
    while rest > 0:
        free = [i for i in range(1, count) if holding[i] < largest] or [i for i in range(1, count) if holding[i] < reach]
        whole, remaining = sum([weights[i] for i in free]), rest
        for i in free:
            more = min(reach - holding[i], max(1, remaining * weights[i] // whole), rest)
            holding[i] = holding[i] + more
            rest = rest - more
    return np.array(holding)


def normal_values(key, extent, width, limit, pieces=(), dtype=jnp.bfloat16):
    drawn = jax.random.normal(key, extent, jnp.float32) * width
    if len(pieces) > 0:
        drawn = shard_levels(key, extent, pieces, -0.22, 0.18) * drawn
    return jnp.clip(drawn, min=-limit, max=limit).astype(dtype)


def setup_inputs(seed: int = 0) -> dict:
    keys = jax.random.split(jax.random.key(seed), 14)
    air_state = normal_values(keys[0], (NVAR, LEV, NCELL), 1.0, 6.0, ((1, 4), (2, 64)), jnp.float32)
    sea_state = normal_values(keys[1], (NVAR, LEV, NCELL), 1.0, 6.0, ((1, 4), (2, 64)), jnp.float32)
    air_courant = jnp.clip(jax.random.uniform(keys[2], (LEV, NCELL), jnp.float32, -0.9, 0.9) * shard_levels(keys[2], (LEV, NCELL), ((0, 4), (1, 64)), -0.4, 0.0), -0.9, 0.9)
    sea_courant = jnp.clip(jax.random.uniform(keys[3], (LEV, NCELL), jnp.float32, -0.9, 0.9) * shard_levels(keys[3], (LEV, NCELL), ((0, 4), (1, 64)), -0.4, 0.0), -0.9, 0.9)
    air_mixing = jnp.clip(jnp.exp(math.log(3.0) - 2.7080502 * jax.random.uniform(keys[4], (LEV, NCELL), jnp.float32) ** shard_levels(keys[4], (LEV, NCELL), ((1, 64),), -0.2, 0.2)), 0.2, 3.0)
    sea_mixing = jnp.clip(jnp.exp(math.log(3.0) - 2.7080502 * jax.random.uniform(keys[5], (LEV, NCELL), jnp.float32) ** shard_levels(keys[5], (LEV, NCELL), ((1, 64),), -0.2, 0.2)), 0.2, 3.0)
    upward_weight = jnp.clip(0.03125 * jax.random.uniform(keys[6], (NBLK, MAP_K, BLOCK * BLOCK), jnp.float32) ** shard_levels(keys[6], (NBLK, MAP_K, BLOCK * BLOCK), ((0, 64),), -0.2, 0.2), 0.0, 0.03125).astype(jnp.bfloat16)
    upward_target_keys = jax.random.split(jax.random.fold_in(keys[7], 1), NBLK // BLK_DEV)
    upward_target_turns = jax.random.permutation(jax.random.fold_in(keys[7], 3), NBLK // BLK_DEV)
    upward_target = jax.vmap(lambda own, number: shared_out(jax.random.fold_in(keys[7], 2), own, number, BLK_DEV, N_TILES, MAP_K, CAP, 2))(upward_target_keys, upward_target_turns).reshape((NBLK, MAP_K))
    upward_block = plant(jax.random.randint(keys[8], (NBLK, MAP_K), 0, BLK_DEV), jax.random.fold_in(keys[8], 1), 0, BLK_DEV - 1).astype(jnp.int32)
    downward_weight = jnp.clip(0.03125 * jax.random.uniform(keys[9], (NBLK, MAP_K, BLOCK * BLOCK), jnp.float32) ** shard_levels(keys[9], (NBLK, MAP_K, BLOCK * BLOCK), ((0, 64),), -0.2, 0.2), 0.0, 0.03125).astype(jnp.bfloat16)
    downward_target_keys = jax.random.split(jax.random.fold_in(keys[10], 1), NBLK // BLK_DEV)
    downward_target_turns = jax.random.permutation(jax.random.fold_in(keys[10], 3), NBLK // BLK_DEV)
    downward_target = jax.vmap(lambda own, number: shared_out(jax.random.fold_in(keys[10], 2), own, number, BLK_DEV, N_TILES, MAP_K, CAP, 2))(downward_target_keys, downward_target_turns).reshape((NBLK, MAP_K))
    downward_block = plant(jax.random.randint(keys[11], (NBLK, MAP_K), 0, BLK_DEV), jax.random.fold_in(keys[11], 1), 0, BLK_DEV - 1).astype(jnp.int32)
    sea_mask = plant((jax.random.randint(keys[12], (NBLK,), 0, 4) < 3).astype(jnp.int32), jax.random.fold_in(keys[12], 1), 0, 1)
    return {"air_state": air_state, "sea_state": sea_state, "air_courant": air_courant, "sea_courant": sea_courant, "air_mixing": air_mixing, "sea_mixing": sea_mixing, "upward_weight": upward_weight, "upward_target": upward_target, "upward_block": upward_block, "downward_weight": downward_weight, "downward_target": downward_target, "downward_block": downward_block, "sea_mask": sea_mask}


def upwind(values, courant):
    left = jnp.roll(values, 1, axis=-1)
    right = jnp.roll(values, -1, axis=-1)
    return values - jnp.maximum(courant, 0.0) * (values - left) - jnp.minimum(courant, 0.0) * (right - values)


def mixing(rhs, coef):
    level_count = rhs.shape[1]
    cprime = []
    dprime = []
    for level in range(level_count):
        upper = coef[level + 1] if level + 1 < level_count else jnp.zeros_like(coef[0])
        if level == 0:
            denom = 1.0 + upper
            value = rhs[:, 0]
        else:
            lower = coef[level]
            denom = 1.0 + lower + upper - lower * cprime[-1]
            value = rhs[:, level] + lower * dprime[-1]
        cprime.append(upper / denom)
        dprime.append(value / denom)
    result = [None] * level_count
    result[-1] = dprime[-1]
    for level in range(level_count - 2, -1, -1):
        result[level] = dprime[level] + cprime[level] * result[level + 1]
    return jnp.stack(result, 1)


def remap(values, weight, target, block_index):
    row_count = values.shape[0]
    matrices = weight.astype(jnp.float32).reshape(weight.shape[0], weight.shape[1], BLOCK, BLOCK)
    contrib = jnp.einsum("okrc,voc->okvr", matrices, values, precision=lax.Precision.HIGHEST)
    where_to = (target * BLK_DEV + block_index).reshape(-1).astype(jnp.int32)
    total = jax.ops.segment_sum(contrib.reshape(-1, row_count, BLOCK), where_to, num_segments=NBLK)
    return jnp.transpose(total, (1, 0, 2)).reshape(row_count, NBLK * BLOCK)


def reference(air_state, sea_state, air_courant, sea_courant, air_mixing, sea_mixing, upward_weight, upward_target, upward_block, downward_weight, downward_target, downward_block, sea_mask):
    air_adv = air_state
    sea_adv = sea_state
    for step in range(ASTEPS):
        air_adv = upwind(air_adv, air_courant[None])
        sea_adv = upwind(sea_adv, sea_courant[None])
    mask_value = sea_mask.astype(jnp.float32)
    source = jnp.concatenate([sea_adv[:, 0, :].reshape(NVAR, NBLK, BLOCK), jnp.ones((1, NBLK, BLOCK), jnp.float32)], 0)
    source = source * mask_value[None, :, None]
    received = remap(source, upward_weight, upward_target, upward_block)
    flux = air_mixing[0] * (received[NVAR] * air_adv[:, 0, :] - received[:NVAR])
    gain = remap(flux.reshape(NVAR, NBLK, BLOCK), downward_weight, downward_target, downward_block)
    gain = gain * jnp.repeat(mask_value, BLOCK)[None]
    air_rhs = air_adv.at[:, 0, :].add(-flux)
    sea_rhs = sea_adv.at[:, 0, :].add(sea_mixing[0] * gain)
    return mixing(air_rhs, air_mixing), mixing(sea_rhs, sea_mixing)
```

```python
import functools

import jax
import jax.numpy as jnp
from jax import lax
from jax.experimental import pallas as pl
from jax.experimental.pallas import tpu as pltpu
from jax.sharding import PartitionSpec as P

BLOCK = 64
LANES = 128
SLOTS = 16
F32 = jnp.float32
BF16 = jnp.bfloat16
NT = (((1,), (1,)), ((), ()))
NN = (((1,), (0,)), ((), ()))


def dot(a, b, dims=NN):
    return lax.dot_general(a, b, dims, preferred_element_type=F32)


def split(x):
    high = x.astype(BF16)
    return high, (x - high.astype(F32)).astype(BF16)


def iota(shape, dim):
    return lax.broadcasted_iota(jnp.int32, shape, dim)


def low_half(shape):
    return iota(shape, len(shape) - 1) < BLOCK


def swap(x):
    return pltpu.roll(x, BLOCK, x.ndim - 1)


class Fetched:
    def __init__(self, source, buf, sem):
        self.copy = pltpu.make_async_copy(source, buf, sem)
        self.shape = source.shape
        self.buf = buf
        self.waiting = True
        self.copy.start()

    def get(self):
        if self.waiting:
            self.copy.wait()
            self.waiting = False
        return self.buf


def onehot(condition):
    return jnp.where(condition, 1.0, 0.0).astype(BF16)


def prepare_kernel(tiles, ut, ub, dt, db, mask, up_out, down_out, label_out, mask_out, order_out):
    blocks = ut.shape[1]
    groups = blocks // 2
    entries = 2 * blocks
    source, lane = iota((blocks, blocks), 0), iota((blocks, blocks), 1)
    turn = onehot(source == 2 * (lane & (groups - 1)) + lane // groups)
    lists = [x.get()[...] for x in (ut, ub, dt, db, mask)]
    stacked = jnp.concatenate([x.astype(F32) for x in lists], 0)
    stacked = jnp.concatenate([stacked, jnp.zeros((16 - stacked.shape[0], blocks), F32)], 0)
    stacked = dot(stacked.astype(BF16), turn)

    def entry_row(at):
        pair = stacked[at : at + 2]
        parts = [
            pair[k : k + 1, odd * groups : (odd + 1) * groups]
            for odd in range(2)
            for k in range(2)
        ]
        return jnp.concatenate(parts, 1)

    tile_row = iota((tiles, entries), 0).astype(F32)
    earlier = onehot(iota((entries, entries), 0) < iota((entries, entries), 1))
    labels = None
    for first, out, base in ((0, up_out, 0), (4, down_out, SLOTS)):
        target, block = entry_row(first), entry_row(first + 2)
        named = jnp.where(target == tile_row, 1.0, 0.0)
        rank = jnp.sum(named * dot(named.astype(BF16), earlier), 0, keepdims=True)
        rank = rank.astype(jnp.int32)
        target = target.astype(jnp.int32)
        rows = tiles * SLOTS // 2
        at = (rank // 2) * tiles + target
        for half in range(2):
            wanted = jnp.where((rank & 1) == half, at, -1)
            out[half] = onehot(iota((rows, entries), 0) == wanted)
        carried = (named * (block + 1.0)).astype(BF16)
        chosen = onehot(iota((LANES, entries), 0) == rank + base)
        term = dot(carried, chosen, NT)
        labels = term if labels is None else labels + term
    label_out[...] = labels
    diagonal = iota((groups, groups), 0) == iota((groups, groups), 1)
    spread = None
    for odd in range(2):
        row = stacked[8:9, odd * groups : (odd + 1) * groups]
        picked = jnp.where(diagonal, row, 0.0).astype(BF16)
        side = onehot((iota((groups, LANES), 1) // BLOCK) == odd)
        term = dot(picked, side)
        spread = term if spread is None else spread + term
    mask_out[...] = spread
    row, column = iota((256, 512), 0), iota((256, 512), 1)
    same = ((row >> 6) & 1) * 2 + (row & 1) == (column >> 7)
    cell = ((row >> 1) & 31) * 2 + (row >> 7)
    order_out[...] = onehot(same & (cell == (column & 63)))


def upwind(x, positive, negative, below, above):
    return x - positive * (x - below) - negative * (above - x)


def surface_kernel(sea, air, sea_c, air_c, o0, o1, o2, o3, first_out, last_out, sbuf, abuf, sems):
    rows = sea_c.shape[0] // 2
    size = 2 * rows
    outs = (o0, o1, o2, o3)
    order = (1, 2, 3, 0)

    def copy(n, d):
        state, buf = ((sea, sbuf), (air, abuf))[n]
        return pltpu.make_async_copy(state.at[pl.ds(d * size, size)], buf.at[d], sems.at[n, d])

    for d in order:
        for n in range(2):
            copy(n, d).start()
    lane = iota((rows, LANES), 1)
    first = lane == 0
    last = lane == LANES - 1
    signs = []
    for n, speed in enumerate((sea_c, air_c)):
        c = speed.get()[pl.ds(0, rows, stride=2), :]
        signs.append((jnp.maximum(c, 0.0), jnp.minimum(c, 0.0)))
    for d in order:
        out = outs[d]
        for n, (buf, speed) in enumerate(((sbuf, sea_c), (abuf, air_c))):
            copy(n, d).wait()
            positive, negative = signs[n]
            x = buf[d, pl.ds(0, rows, stride=2), :]
            for step in range(2):
                below = pltpu.roll(x, 1, 1)
                below = jnp.where(first, pltpu.roll(below, 1, 0), below)
                above = pltpu.roll(x, LANES - 1, 1)
                above = jnp.where(last, pltpu.roll(above, rows - 1, 0), above)
                x = upwind(x, positive, negative, below, above)
            out[n * rows : (n + 1) * rows, :] = x
            at = 2 * rows + n
            out[at : at + 1, :] = buf[d, 0:1, :]
            out[at + 2 : at + 3, :] = speed.get()[0:1, :]
            out[at + 4 : at + 5, :] = buf[d, size - 2 : size - 1, :]
            out[at + 6 : at + 7, :] = speed.get()[size - 2 : size - 1, :]
            at = n * 10 + 2 * d
            first_out[at : at + 2, :] = buf[d, 0:2, :]
            last_out[at : at + 2, :] = buf[d, size - 2 : size, :]
    for n, speed in enumerate((sea_c, air_c)):
        at = n * 10 + 8
        first_out[at : at + 2, :] = speed.get()[0:2, :]
        last_out[at : at + 2, :] = speed.get()[size - 2 : size, :]


def advect_kernel(
    fields, sea, air, sea_c, air_c, left, right, lev, o0, o1, o2, o3, xbuf, cbuf
):
    rows = sea_c.shape[0] // 2
    total = rows + 16
    lane = iota((total, LANES), 1)
    first = lane == 0
    last = lane == LANES - 1

    def extended(buf, middle, at):
        buf[0:8, :] = jnp.broadcast_to(left.get()[pl.ds(at, 1), :], (8, LANES))
        buf[8 : rows + 8, :] = middle
        buf[rows + 8 :, :] = jnp.broadcast_to(right.get()[pl.ds(at, 1), :], (8, LANES))
        return buf[...]

    for n, (state, courant) in enumerate(((sea, sea_c), (air, air_c))):
        for level in range(2):
            c = courant.get()[pl.ds(level, rows, stride=2), :]
            c = extended(cbuf, c, n * 10 + 8 + level)
            positive, negative = jnp.maximum(c, 0.0), jnp.minimum(c, 0.0)
            for d, out in enumerate((o0, o1, o2, o3)):
                field = lax.rem(lev[0] + d, fields)
                at = field * 2 * rows + level
                x = state.get()[pl.ds(at, rows, stride=2), :]
                x = extended(xbuf, x, n * 10 + 2 * field + level)
                for step in range(2):
                    below = pltpu.roll(x, 1, 1)
                    below = jnp.where(first, pltpu.roll(below, 1, 0), below)
                    above = pltpu.roll(x, LANES - 1, 1)
                    above = jnp.where(last, pltpu.roll(above, total - 1, 0), above)
                    x = upwind(x, positive, negative, below, above)
                at = (2 * n + level) * rows
                out[at : at + rows, :] = x[8 : rows + 8, :]


def mended(ends, left, right):
    low = low_half((2, LANES))
    out = []
    for at, outer, kept in ((0, left, low), (4, right, jnp.logical_not(low))):
        x = jnp.where(kept, ends[at : at + 2, :], outer[4 - at : 6 - at, :])
        c = jnp.where(kept, ends[at + 2 : at + 4, :], outer[6 - at : 8 - at, :])
        positive, negative = jnp.maximum(c, 0.0), jnp.minimum(c, 0.0)
        for step in range(2):
            x = upwind(x, positive, negative, pltpu.roll(x, 1, 1), pltpu.roll(x, LANES - 1, 1))
        out.append(x)
    return out


def mend(row, mended_row, at_end):
    lane = iota(row.shape, 1)
    return jnp.where(lane >= LANES - 2 if at_end else lane < 2, mended_row, row)


def weight_copies(weight, wbuf, sems):
    pieces = sems.shape[0]
    size = weight.shape[0] // pieces
    return [
        pltpu.make_async_copy(
            weight.at[pl.ds(n * size, size)], wbuf.at[pl.ds(n * size, size)], sems.at[n]
        )
        for n in range(pieces)
    ]


def product_rows(values, ones, put):
    half = low_half(values.shape)
    zero = jnp.zeros(values.shape, F32)
    high = values.astype(BF16).astype(F32)
    sets = [(0, 2, high), (2, 2, values - high)]
    if ones is not None:
        sets.append((8, 0, ones))
    for base, gap, x in sets:
        turned = swap(x)
        for odd in range(2):
            for parity in range(2):
                row = base + odd * (2 + gap) + parity
                chosen = turned if odd != parity else x
                put(row, jnp.where(half == (parity == 0), chosen, zero))
    if ones is not None:
        for row in range(12, 16):
            put(row, zero)


def product_sums(got, with_ones):
    half = low_half(got(0).shape)
    out = [jnp.where(half, got(p) + got(2 + p), got(4 + p) + got(6 + p)) for p in range(2)]
    if with_ones:
        out.extend(jnp.where(half, got(8 + p), got(10 + p)) for p in range(2))
    return out


def products(values, ones, copies, wbuf, lhs, res):
    groups = values.shape[0]
    count = 8 if ones is None else 16

    def put(row, x):
        lhs[pl.ds(row, groups, stride=count), :] = x

    product_rows(values, ones, put)

    def body(g, carry):
        at = pl.ds(pl.multiple_of(g * count, count), count)
        w = wbuf[pl.ds(pl.multiple_of(g * LANES, LANES), LANES), :]
        res[at, :] = dot(lhs[at, :].astype(BF16), w, NT)
        return carry

    each = groups // len(copies)
    for n, copy in enumerate(copies):
        copy.wait()
        lax.fori_loop(n * each, (n + 1) * each, body, 0, unroll=8)
    return product_sums(lambda row: res[pl.ds(row, groups, stride=count), :], ones is not None)


def entry_values(sums, order):
    def ordered(pair):
        high, low = split(jnp.concatenate(pair, 1))
        return dot(high, order), dot(low, order)

    y = ordered(sums[:2])
    if len(sums) > 2:
        half = low_half(y[0].shape[:1] + (LANES,))
        half = jnp.concatenate([half] * 4, 1)
        y = [jnp.where(half, a, b) for a, b in zip(y, ordered(sums[2:]))]
    terms = []
    for part in y:
        part = part.astype(BF16)
        terms.append(jnp.concatenate([part[:, q * LANES : (q + 1) * LANES] for q in range(4)], 0))
    return jnp.concatenate(terms, 1)


def dispatched(place, entries):
    out = []
    for half in range(2):
        slots = dot(place[half], entries)
        out.append(slots[:, :LANES] + slots[:, LANES:])
    return out


def up_kernel(surface, mask, weight, sums_out, wbuf, lhs, res, wsems):
    groups = mask.shape[0]
    copies = weight_copies(weight, wbuf, wsems)
    for copy in copies:
        copy.start()
    mask_value = mask.get()[...]
    values = surface.get()[0:groups, :] * mask_value
    sums = products(values, mask_value, copies, wbuf, lhs, res)
    sums_out[...] = jnp.concatenate(sums, 1)


def slot_kernel(
    sums, surface, left, right, mask, weight, place, order, labels, out, wbuf, lhs, sems
):
    groups = mask.shape[0]
    tiles = labels.shape[0]
    copies = [
        pltpu.make_async_copy(weight.at[pl.ds(at, LANES)], wbuf.at[n], sems.at[n])
        for n, at in enumerate((0, (groups - 1) * LANES))
    ]
    for copy in copies:
        copy.start()
    surface, mask, sums = surface.get(), mask.get(), sums.get()
    mended_rows = mended(
        surface[2 * groups : 2 * groups + 8, :], left.get()[...], right.get()[...]
    )
    row_at = iota((groups, LANES), 0)
    parts = [sums[:, n * LANES : (n + 1) * LANES] for n in range(4)]
    for n, g in enumerate((0, groups - 1)):
        row = surface[g : g + 1, :]
        row = mend(row, mended_rows[n][0:1], n == 1) * mask[g : g + 1, :]

        def put(at, x):
            lhs[at : at + 1, :] = x

        product_rows(row, None, put)
        copies[n].wait()
        res = dot(lhs[...].astype(BF16), wbuf[n], NT)
        for p, new in enumerate(product_sums(lambda at: res[at : at + 1], False)):
            parts[p] = jnp.where(row_at == g, new, parts[p])
    even, odd = dispatched(place.get(), entry_values(parts, order.get()[...]))
    half = low_half((tiles, LANES))
    pitch = out.shape[0] // tiles
    for i in range(SLOTS // 2):
        a, b = even[i * tiles : (i + 1) * tiles], odd[i * tiles : (i + 1) * tiles]
        out[pl.ds(i, tiles, stride=pitch), :] = jnp.where(half, a, swap(b))
        out[pl.ds(SLOTS // 2 + i, tiles, stride=pitch), :] = jnp.where(half, swap(a), b)
    out[pl.ds(SLOTS, tiles, stride=pitch), :] = labels.get()[...]


def named_blocks(labels, base, blocks):
    turned = jnp.transpose(jnp.concatenate([labels, labels], 0))
    half = low_half((1, LANES))
    out = []
    for slot_half in range(2):
        row = []
        for i in range(0, SLOTS // 2, 2):
            at = base + 2 * i + slot_half
            row.append(jnp.where(half, turned[at : at + 1], turned[at + 2 : at + 3]))
        row = jnp.concatenate(row, 1).astype(jnp.int32)
        for odd in range(2):
            out.append(onehot(2 * iota((blocks, row.shape[1]), 0) + odd + 1 == row))
    return out


def collected(parts, names):
    halves = []
    for part in parts:
        halves.extend(split(part))
    values = jnp.concatenate(halves, 1)
    sums = [dot(name, values) for name in names]
    half = low_half((sums[0].shape[0], LANES))
    out = []
    for n in range(len(parts)):
        at = 2 * n * LANES
        g = [s[:, at : at + LANES] + s[:, at + LANES : at + 2 * LANES] for s in sums]
        out.append(jnp.where(half, g[0] + swap(g[2]), swap(g[1]) + g[3]))
    return out


def slot_rows(arrived, start, count, tiles):
    pitch = arrived.shape[0] // tiles
    return jnp.concatenate(
        [arrived[pl.ds(start + i, tiles, stride=pitch), :] for i in range(count)], 0
    )


def middle_kernel(
    arrived, surface, left, right, mixing, weight, place, order,
    flux_out, out, label_out, wbuf, lhs, res, wsems,
):
    groups = flux_out.shape[0]
    tiles = label_out.shape[0]
    copies = weight_copies(weight, wbuf, wsems)
    for copy in copies:
        copy.start()
    labels = arrived[pl.ds(SLOTS, tiles, stride=SLOTS + 1), :]
    label_out[...] = labels
    names = named_blocks(labels, 0, groups)
    field = slot_rows(arrived, 0, SLOTS // 2, tiles)
    cover = slot_rows(arrived, SLOTS // 2, SLOTS // 2, tiles)
    received, coverage = collected((field, cover), names)
    surface = surface.get()
    mended_rows = mended(
        surface[2 * groups : 2 * groups + 8, :], left.get()[...], right.get()[...]
    )
    for n, at in enumerate((groups, 2 * groups - 1)):
        surface[at : at + 1, :] = mend(surface[at : at + 1, :], mended_rows[n][1:2], n == 1)
    factor = mixing.get()[pl.ds(0, groups, stride=8), :]
    flux = factor * (coverage * surface[groups : 2 * groups, :] - received)
    flux_out[...] = flux
    sums = products(flux, None, copies, wbuf, lhs, res)
    even, odd = dispatched(place.get(), entry_values(sums, order.get()[...]))
    half = low_half((tiles, LANES))
    pitch = out.shape[0] // tiles
    for i in range(SLOTS // 2):
        a, b = even[i * tiles : (i + 1) * tiles], odd[i * tiles : (i + 1) * tiles]
        out[pl.ds(i, tiles, stride=pitch), :] = jnp.where(half, a, b)


def solve_kernel(with_flux, p0, p1, p2, p3, mixing, extra, lev, *refs):
    if with_flux:
        out, buf, sems = refs
    else:
        out, unit_out, buf, sems = refs
    groups = extra.shape[0]
    chunk = 16
    levels = 8
    base = 2 * groups if with_flux else 0
    copies = []
    for d, part in enumerate((p0, p1, p2, p3)):
        source = lax.rem(lev[0] + 4 - d, 4)
        copies.append(
            pltpu.make_async_copy(
                part.at[pl.ds(base, 2 * groups)], buf.at[source], sems.at[d]
            )
        )
    for copy in copies:
        copy.start()
    kbuf, ebuf = mixing.get(), extra.get()
    for copy in copies:
        copy.wait()

    def body(step, carry):
        at = pl.multiple_of(step * chunk, chunk)
        rows = pl.ds(at, chunk)
        k = [
            kbuf[pl.ds(at * levels + level, chunk, stride=levels), :] for level in range(levels)
        ]
        cs, ds, es = [], [], []
        for level in range(levels):
            r = buf[level // 2, pl.ds((level % 2) * groups + at, chunk), :]
            if level == 0:
                inverse = 1.0 / (1.0 + k[1])
                if with_flux:
                    r = r - ebuf[rows, :]
                else:
                    es.append(k[0] * ebuf[rows, :] * inverse)
                ds.append(r * inverse)
            else:
                total = 1.0 + k[level] - k[level] * cs[-1]
                if level + 1 < levels:
                    total = total + k[level + 1]
                inverse = 1.0 / total
                ds.append((r + k[level] * ds[-1]) * inverse)
                if not with_flux:
                    es.append(k[level] * es[-1] * inverse)
            if level + 1 < levels:
                cs.append(k[level + 1] * inverse)
        for terms, ref in ((ds, out),) if with_flux else ((ds, out), (es, unit_out)):
            x = terms[-1]
            ref[pl.ds(at * levels + levels - 1, chunk, stride=levels), :] = x
            for level in range(levels - 2, -1, -1):
                x = terms[level] + cs[level] * x
                ref[pl.ds(at * levels + level, chunk, stride=levels), :] = x
        return carry

    lax.fori_loop(0, groups // chunk, body, 0)


def last_kernel(arrived, labels, base, unit, out, gain):
    tiles = labels.shape[0]
    groups = gain.shape[0]
    names = named_blocks(labels.get()[...], SLOTS, groups)
    (total,) = collected((slot_rows(arrived, 0, SLOTS // 2, tiles),), names)
    gain[...] = total
    bbuf, ubuf = base.get(), unit.get()

    def body(step, carry):
        at = pl.ds(pl.multiple_of(step * 8, 8), 8)
        out[at, :] = bbuf[at, :] + ubuf[at, :] * gain[pl.ds(step, 1), :]
        return carry

    lax.fori_loop(0, groups, body, 0, unroll=8)


VMEM = pl.BlockSpec(memory_space=pltpu.VMEM)
SMEM = pl.BlockSpec(memory_space=pltpu.SMEM)
HBM = pl.BlockSpec(memory_space=pltpu.HBM)
DMA = pltpu.SemaphoreType.DMA


def call(kernel, shapes, args, spaces, scratch=(), name=None, us=1.0, after=()):
    fetched = [i for i, space in enumerate(spaces) if space == "f"]
    outs = len(shapes) if isinstance(shapes, tuple) else 1

    def body(*refs):
        refs = list(refs)
        del refs[len(args) : len(args) + len(after)]
        end = len(refs) - 2 * len(fetched)
        for n, i in enumerate(fetched):
            refs[i] = Fetched(refs[i], refs[end + n], refs[end + len(fetched) + n])
        kernel(*refs[:end])

    extra = [pltpu.VMEM(args[i].shape, args[i].dtype) for i in fetched]
    extra += [DMA(()) for i in fetched]
    return pl.pallas_call(
        body,
        out_shape=shapes,
        in_specs=[{"v": VMEM, "s": SMEM, "h": HBM, "f": HBM}[space] for space in spaces]
        + [HBM] * len(after),
        out_specs=jax.tree.map(lambda _: VMEM, shapes),
        scratch_shapes=list(scratch) + extra,
        compiler_params=pltpu.CompilerParams(vmem_limit_bytes=64 * 1024 * 1024),
        cost_estimate=pl.CostEstimate(
            flops=0, bytes_accessed=int(us * 3.6e6), transcendentals=0
        ),
        name=name,
    )(*args, *after)


def shape(*dims, dtype=F32):
    return jax.ShapeDtypeStruct(dims, dtype)


def tile_rows(x, lead):
    levels, cells = x.shape[-2:]
    x = x.reshape(lead, levels, cells // LANES, LANES)
    return x.transpose(0, 2, 1, 3).reshape(lead * levels * cells // LANES, LANES)


def weight_rows(w):
    blocks, fan, size = w.shape
    w = w.reshape(blocks, fan, size // LANES, LANES).transpose(0, 2, 1, 3)
    return w.reshape(blocks * fan * size // LANES, LANES)


def on_device(
    air_state,
    sea_state,
    air_courant,
    sea_courant,
    air_mixing,
    sea_mixing,
    upward_weight,
    upward_target,
    upward_block,
    downward_weight,
    downward_target,
    downward_block,
    sea_mask,
):
    fields, pair, cells = air_state.shape
    tiles = lax.axis_size("tiles")
    levs = lax.axis_size("lev")
    rows = cells // LANES
    groups = sea_mask.shape[0] // 2
    lev = lax.axis_index("lev").astype(jnp.int32)
    lev_ref = lev.reshape(1)
    forward = [(i, (i + 1) % tiles) for i in range(tiles)]
    backward = [(b, a) for a, b in forward]
    states = (
        tile_rows(sea_state, fields),
        tile_rows(air_state, fields),
        tile_rows(sea_courant, 1),
        tile_rows(air_courant, 1),
    )
    size = pair * rows

    *parts, rest_first, rest_last = call(
        surface_kernel,
        tuple(shape(size + 8, LANES) for _ in range(4)) + (shape(20, LANES),) * 2,
        states,
        "hhff",
        scratch=[
            pltpu.VMEM((4, size, LANES), F32),
            pltpu.VMEM((4, size, LANES), F32),
            DMA((2, 4)),
        ],
        name="surface",
        us=3.0,
    )
    moved = [lax.ppermute(parts[d], "lev", [(0, d)]) for d in range(1, levs)]
    surface = jnp.where(lev == 0, parts[0], moved[0] + moved[1] + moved[2])
    ends = surface[size:]
    left = lax.ppermute(ends, "tiles", forward)
    right = lax.ppermute(ends, "tiles", backward)
    rest_left = lax.ppermute(rest_last, "tiles", forward)
    rest_right = lax.ppermute(rest_first, "tiles", backward)

    places = tiles * SLOTS // 2
    entries = 4 * groups
    place_up, place_down, labels, mask, order = call(
        functools.partial(prepare_kernel, tiles),
        (
            shape(2, places, entries, dtype=BF16),
            shape(2, places, entries, dtype=BF16),
            shape(tiles, LANES),
            shape(groups, LANES),
            shape(256, 512, dtype=BF16),
        ),
        (
            upward_target.T,
            upward_block.T,
            downward_target.T,
            downward_block.T,
            sea_mask.reshape(1, -1),
        ),
        "fffff",
        name="prepare",
        us=3.0,
        after=(parts[0],),
    )
    air_k = tile_rows(air_mixing, 1)
    sea_k = tile_rows(sea_mixing, 1)
    up_rows = weight_rows(upward_weight)
    down_rows = weight_rows(downward_weight)

    def workspace(count):
        return [
            pltpu.VMEM(up_rows.shape, BF16),
            pltpu.VMEM((groups * count, LANES), F32),
            pltpu.VMEM((groups * count, LANES), F32),
        ]

    sums = call(
        up_kernel,
        shape(groups, 4 * LANES),
        (surface, mask, up_rows),
        "ffh",
        scratch=[*workspace(16), DMA((8,))],
        name="upward",
        us=5.0,
        after=(rest_left, rest_right),
    )
    pitch = SLOTS + 1
    outgoing = call(
        slot_kernel,
        shape(tiles * pitch, LANES),
        (sums, surface, left, right, mask, up_rows, place_up, order, labels),
        "fffffhfff",
        scratch=[
            pltpu.VMEM((2, LANES, LANES), BF16),
            pltpu.VMEM((8, LANES), F32),
            DMA((2,)),
        ],
        name="to_slots",
        us=2.0,
    )

    def over_tiles(x):
        y = x.reshape(tiles, 1, x.size // tiles)
        y = lax.all_to_all(y, "tiles", split_axis=0, concat_axis=0, tiled=True)
        return y.reshape(x.shape)

    rest = call(
        functools.partial(advect_kernel, fields),
        tuple(shape(2 * size, LANES) for _ in range(4)),
        (*states, rest_left, rest_right, lev_ref),
        "ffffffs",
        scratch=[pltpu.VMEM((rows + 16, LANES), F32)] * 2,
        name="advect",
        us=3.0,
        after=(outgoing,),
    )
    rest = [rest[0]] + [
        lax.ppermute(rest[d], "lev", [(i, (i + d) % levs) for i in range(levs)])
        for d in range(1, levs)
    ]
    arrived = over_tiles(outgoing)
    flux, returning, labels_down = call(
        middle_kernel,
        (shape(groups, LANES), shape(tiles * SLOTS // 2, LANES), shape(tiles, LANES)),
        (arrived, surface, left, right, air_k, down_rows, place_down, order),
        "vffffhff",
        scratch=[*workspace(8), DMA((8,))],
        name="middle",
        us=7.0,
        after=tuple(rest[1:]),
    )
    gained = over_tiles(returning)

    column = shape(8 * rows, LANES)

    def solve(with_flux, k, extra, name):
        return call(
            functools.partial(solve_kernel, with_flux),
            column if with_flux else (column, column),
            (*rest, k, extra, lev_ref),
            "hhhhffs",
            scratch=[pltpu.VMEM((4, size, LANES), F32), DMA((4,))],
            name=name,
            us=2.0,
        )

    base, unit = solve(False, sea_k, mask, "solve_sea")
    air_out = solve(True, air_k, flux, "solve_air")
    sea_out = call(
        last_kernel,
        column,
        (gained, labels_down, base, unit),
        "vfff",
        scratch=[pltpu.VMEM((rows, LANES), F32)],
        name="last",
        us=2.0,
    )

    def levels_first(x):
        return x.reshape(rows, 8, LANES).transpose(1, 0, 2).reshape(1, 8, cells)

    return levels_first(air_out), levels_first(sea_out)


def solution(mesh):
    return jax.shard_map(
        on_device,
        mesh=mesh,
        in_specs=(
            P(None, "lev", "tiles"),
            P(None, "lev", "tiles"),
            P("lev", "tiles"),
            P("lev", "tiles"),
            P(None, "tiles"),
            P(None, "tiles"),
            P("tiles", None, None),
            P("tiles", None),
            P("tiles", None),
            P("tiles", None, None),
            P("tiles", None),
            P("tiles", None),
            P("tiles"),
        ),
        out_specs=(P("lev", None, "tiles"), P("lev", None, "tiles")),
        check_vma=False,
    )
```

```python
import functools

import jax
import jax.numpy as jnp
from jax import lax
from jax.experimental import pallas as pl
from jax.experimental.pallas import tpu as pltpu
from jax.sharding import PartitionSpec as P

BLOCK = 64
LANES = 128
SLOTS = 16
PIECES = 4
AHEAD = 2
F32 = jnp.float32
BF16 = jnp.bfloat16
NT = (((1,), (1,)), ((), ()))
NN = (((1,), (0,)), ((), ()))


def dot(a, b, dims=NN):
    return lax.dot_general(a, b, dims, preferred_element_type=F32)


def split(x):
    high = x.astype(BF16)
    return high, (x - high.astype(F32)).astype(BF16)


def iota(shape, dim):
    return lax.broadcasted_iota(jnp.int32, shape, dim)


def low_half(shape):
    return iota(shape, len(shape) - 1) < BLOCK


def swap(x):
    return pltpu.roll(x, BLOCK, x.ndim - 1)


class Fetched:
    def __init__(self, source, buf, sem):
        self.copy = pltpu.make_async_copy(source, buf, sem)
        self.shape = source.shape
        self.buf = buf
        self.waiting = True
        self.copy.start()

    def get(self):
        if self.waiting:
            self.copy.wait()
            self.waiting = False
        return self.buf


def onehot(condition):
    return jnp.where(condition, 1.0, 0.0).astype(BF16)


def prepare_kernel(tiles, ut, ub, dt, db, mask, up_out, down_out, label_out, mask_out):
    blocks = ut.shape[1]
    groups = blocks // 2
    entries = 2 * blocks
    source, lane = iota((blocks, blocks), 0), iota((blocks, blocks), 1)
    turn = onehot(source == 2 * (lane & (groups - 1)) + lane // groups)
    lists = [x.get()[...] for x in (ut, ub, dt, db, mask)]
    stacked = jnp.concatenate([x.astype(F32) for x in lists], 0)
    stacked = jnp.concatenate([stacked, jnp.zeros((16 - stacked.shape[0], blocks), F32)], 0)
    stacked = dot(stacked.astype(BF16), turn)

    def entry_row(at):
        pair = stacked[at : at + 2]
        parts = [
            pair[k : k + 1, odd * groups : (odd + 1) * groups]
            for odd in range(2)
            for k in range(2)
        ]
        return jnp.concatenate(parts, 1)

    tile_row = iota((tiles, entries), 0).astype(F32)
    earlier = onehot(iota((entries, entries), 0) < iota((entries, entries), 1))
    labels = None
    for first, out, base in ((0, up_out, 0), (4, down_out, SLOTS)):
        target, block = entry_row(first), entry_row(first + 2)
        named = jnp.where(target == tile_row, 1.0, 0.0)
        rank = jnp.sum(named * dot(named.astype(BF16), earlier), 0, keepdims=True)
        rank = rank.astype(jnp.int32)
        target = target.astype(jnp.int32)
        at = (rank // 2) * tiles + target
        for half in range(2):
            out[half : half + 1, :] = jnp.where((rank & 1) == half, at, -1)
        carried = (named * (block + 1.0)).astype(BF16)
        chosen = onehot(iota((LANES, entries), 0) == rank + base)
        term = dot(carried, chosen, NT)
        labels = term if labels is None else labels + term
    label_out[...] = labels
    diagonal = iota((groups, groups), 0) == iota((groups, groups), 1)
    spread = None
    for odd in range(2):
        row = stacked[8:9, odd * groups : (odd + 1) * groups]
        picked = jnp.where(diagonal, row, 0.0).astype(BF16)
        side = onehot((iota((groups, LANES), 1) // BLOCK) == odd)
        term = dot(picked, side)
        spread = term if spread is None else spread + term
    mask_out[...] = spread


def edge_kernel(sea, air, sea_c, air_c, place, pair_out, next_out, first, last, sems):
    fields = 4
    copies = []
    for n, (state, courant) in enumerate(((sea, sea_c), (air, air_c))):
        size = courant.shape[0]
        for at in range(fields + 1):
            source, base = (state, at * size) if at < fields else (courant, 0)
            for side, (buf, start) in enumerate(((first, 0), (last, size - 8))):
                copies.append(
                    pltpu.make_async_copy(
                        source.at[pl.ds(base + start, 8)], buf.at[n, at], sems.at[n, at, side]
                    )
                )
    for copy in copies:
        copy.start()
    for copy in copies:
        copy.wait()
    for n in range(2):
        for at in range(fields + 1):
            row = n * 2 * (fields + 1) + 2 * at
            low, high = first[n, at, 0:2, :], last[n, at, 6:8, :]
            pair_out[row : row + 2, :] = jnp.where(place[0] // 4 == 0, high, low)
            next_out[row : row + 2, :] = jnp.where(place[0] // 4 == 0, low, high)


def neighbours(pair, other, place):
    pair, other = pair.get()[...], other.get()[...]
    even = place[0] // 4 == 0
    return jnp.where(even, other, pair), jnp.where(even, pair, other)


def stepped(x, low, high, positive, negative, buf):
    rows = x.shape[0]
    total = buf.shape[0]
    lane = iota((total, LANES), 1)
    first = lane == 0
    last = lane == LANES - 1
    buf[0:8, :] = jnp.broadcast_to(low, (8, LANES))
    buf[8 : rows + 8, :] = x
    buf[rows + 8 :, :] = jnp.broadcast_to(high, (8, LANES))
    x = buf[...]
    for step in range(2):
        below = pltpu.roll(x, 1, 1)
        below = jnp.where(first, pltpu.roll(below, 1, 0), below)
        above = pltpu.roll(x, LANES - 1, 1)
        above = jnp.where(last, pltpu.roll(above, total - 1, 0), above)
        x = x - positive * (x - below) - negative * (above - x)
    return x[8 : rows + 8, :]


def speeds(c, low, high, buf):
    rows = c.shape[0]
    buf[0:8, :] = jnp.broadcast_to(low, (8, LANES))
    buf[8 : rows + 8, :] = c
    buf[rows + 8 :, :] = jnp.broadcast_to(high, (8, LANES))
    c = buf[...]
    return jnp.maximum(c, 0.0), jnp.minimum(c, 0.0)


def surface_kernel(sea, sea_c, pair, other, place, o0, o1, o2, o3, sbuf, xbuf, cbuf, sems):
    rows = sea_c.shape[0] // 2
    size = 2 * rows
    outs = (o0, o1, o2, o3)
    order = (1, 2, 3, 0)

    def copy(d):
        return pltpu.make_async_copy(sea.at[pl.ds(d * size, size)], sbuf.at[d], sems.at[d])

    for d in order:
        copy(d).start()
    left, right = neighbours(pair, other, place)
    c = sea_c.get()[pl.ds(0, rows, stride=2), :]
    positive, negative = speeds(c, left[8:9, :], right[8:9, :], cbuf)
    for d in order:
        copy(d).wait()
        x = sbuf[d, pl.ds(0, rows, stride=2), :]
        low, high = left[2 * d : 2 * d + 1, :], right[2 * d : 2 * d + 1, :]
        outs[d][...] = stepped(x, low, high, positive, negative, xbuf)


def advect_kernel(
    fields, base, state, courant, pair, other, lev, o0, o1, o2, o3, lows, highs, xbuf, cbuf
):
    rows = courant.shape[0] // 2
    lows[...], highs[...] = neighbours(pair, other, lev)
    for level in range(2):
        c = courant.get()[pl.ds(level, rows, stride=2), :]
        at = base + 8 + level
        positive, negative = speeds(c, lows[at : at + 1, :], highs[at : at + 1, :], cbuf)
        for d, out in enumerate((o0, o1, o2, o3)):
            field = lax.rem(lev[0] + d, fields)
            x = state.get()[pl.ds(field * 2 * rows + level, rows, stride=2), :]
            at = pl.ds(base + 2 * field + level, 1)
            x = stepped(x, lows[at, :], highs[at, :], positive, negative, xbuf)
            out[level * rows : (level + 1) * rows, :] = x


def weight_copies(weight, wbuf, sems):
    pieces = sems.shape[0]
    size = weight.shape[0] // pieces
    return [
        pltpu.make_async_copy(
            weight.at[pl.ds(n * size, size)], wbuf.at[pl.ds(n * size, size)], sems.at[n]
        )
        for n in range(pieces)
    ]


def product_rows(values, ones, put):
    half = low_half(values.shape)
    zero = jnp.zeros(values.shape, F32)
    high = values.astype(BF16).astype(F32)
    sets = [(0, 2, high), (2, 2, values - high)]
    if ones is not None:
        sets.append((8, 0, ones))
    for base, gap, x in sets:
        turned = swap(x)
        for odd in range(2):
            for parity in range(2):
                row = base + odd * (2 + gap) + parity
                chosen = turned if odd != parity else x
                put(row, jnp.where(half == (parity == 0), chosen, zero))
    if ones is not None:
        for row in range(12, 16):
            put(row, zero)


def product_sums(got, with_ones):
    half = low_half(got(0).shape)
    out = [jnp.where(half, got(p) + got(2 + p), got(4 + p) + got(6 + p)) for p in range(2)]
    if with_ones:
        out.extend(jnp.where(half, got(8 + p), got(10 + p)) for p in range(2))
    return out


def products(values, ones, copies, wbuf, lhs, res):
    groups = values.shape[0]
    count = 8 if ones is None else 16

    def put(row, x):
        lhs[pl.ds(row, groups, stride=count), :] = x

    product_rows(values, ones, put)

    def body(step, carry):
        w = wbuf[pl.ds(pl.multiple_of(step * 2 * LANES, 2 * LANES), 2 * LANES), :]
        both = pl.ds(pl.multiple_of(step * 2 * count, 2 * count), 2 * count)
        out = dot(lhs[both, :].astype(BF16), w, NT)
        for n in range(2):
            at = pl.ds(pl.multiple_of((2 * step + n) * count, count), count)
            res[at, :] = out[n * count : (n + 1) * count, n * LANES : (n + 1) * LANES]
        return carry

    each = groups // 2 // len(copies)
    for n, copy in enumerate(copies):
        copy.wait()
        if n + AHEAD < len(copies):
            copies[n + AHEAD].start()
        lax.fori_loop(n * each, (n + 1) * each, body, 0, unroll=each)
    return product_sums(lambda row: res[pl.ds(row, groups, stride=count), :], ones is not None)


def entry_values(sums):
    row, column = iota((256, 512), 0), iota((256, 512), 1)
    same = ((row >> 6) & 1) * 2 + (row & 1) == (column >> 7)
    cell = ((row >> 1) & 31) * 2 + (row >> 7)
    order = onehot(same & (cell == (column & 63)))

    def ordered(pair):
        high, low = split(jnp.concatenate(pair, 1))
        return dot(high, order), dot(low, order)

    y = ordered(sums[:2])
    if len(sums) > 2:
        half = low_half(y[0].shape[:1] + (LANES,))
        half = jnp.concatenate([half] * 4, 1)
        y = [jnp.where(half, a, b) for a, b in zip(y, ordered(sums[2:]))]
    terms = []
    for part in y:
        part = part.astype(BF16)
        terms.append(jnp.concatenate([part[:, q * LANES : (q + 1) * LANES] for q in range(4)], 0))
    return jnp.concatenate(terms, 1)


def dispatched(place, entries):
    count = entries.shape[0]
    out = []
    for half in range(2):
        chosen = onehot(iota((count, count), 0) == place[half : half + 1, :])
        slots = dot(chosen, entries)
        out.append(slots[:, :LANES] + slots[:, LANES:])
    return out


def surface_copy(parts, at, lev, buf, sem):
    copies = [
        pltpu.make_async_copy(part.at[pl.ds(at, buf.shape[0])], buf, sem) for part in parts
    ]
    for d, copy in enumerate(copies):

        @pl.when(lev[0] % 4 == d)
        def start(copy=copy):
            copy.start()

    return copies[0]


def up_kernel(
    p0, p1, p2, p3, mask, place, labels, weight, lev, out, values, wbuf, lhs, res, sem, wsems
):
    tiles = labels.shape[0]
    field = surface_copy((p0, p1, p2, p3), 0, lev, values, sem)
    copies = weight_copies(weight, wbuf, wsems)
    for copy in copies[:AHEAD]:
        copy.start()
    field.wait()
    mask_value = mask.get()[...]
    sums = products(values[...] * mask_value, mask_value, copies, wbuf, lhs, res)
    even, odd = dispatched(place.get(), entry_values(sums))
    half = low_half((tiles, LANES))
    pitch = out.shape[0] // tiles
    for i in range(SLOTS // 2):
        a, b = even[i * tiles : (i + 1) * tiles], odd[i * tiles : (i + 1) * tiles]
        out[pl.ds(i, tiles, stride=pitch), :] = jnp.where(half, a, swap(b))
        out[pl.ds(SLOTS // 2 + i, tiles, stride=pitch), :] = jnp.where(half, swap(a), b)
    out[pl.ds(SLOTS, tiles, stride=pitch), :] = labels.get()[...]


def named_blocks(labels, base, blocks):
    turned = jnp.transpose(jnp.concatenate([labels, labels], 0))
    half = low_half((1, LANES))
    out = []
    for slot_half in range(2):
        row = []
        for i in range(0, SLOTS // 2, 2):
            at = base + 2 * i + slot_half
            row.append(jnp.where(half, turned[at : at + 1], turned[at + 2 : at + 3]))
        row = jnp.concatenate(row, 1).astype(jnp.int32)
        for odd in range(2):
            out.append(onehot(2 * iota((blocks, row.shape[1]), 0) + odd + 1 == row))
    return out


def collected(parts, names):
    halves = []
    for part in parts:
        halves.extend(split(part))
    values = jnp.concatenate(halves, 1)
    sums = [dot(name, values) for name in names]
    half = low_half((sums[0].shape[0], LANES))
    out = []
    for n in range(len(parts)):
        at = 2 * n * LANES
        g = [s[:, at : at + LANES] + s[:, at + LANES : at + 2 * LANES] for s in sums]
        out.append(jnp.where(half, g[0] + swap(g[2]), swap(g[1]) + g[3]))
    return out


def slot_rows(arrived, start, count, tiles):
    pitch = arrived.shape[0] // tiles
    return jnp.concatenate(
        [arrived[pl.ds(start + i, tiles, stride=pitch), :] for i in range(count)], 0
    )


def middle_kernel(
    arrived, p0, p1, p2, p3, mixing, place, weight, lev,
    flux_out, out, label_out, values, wbuf, lhs, res, sem, wsems,
):
    groups = flux_out.shape[0]
    tiles = label_out.shape[0]
    surface = surface_copy((p0, p1, p2, p3), 0, lev, values, sem)
    copies = weight_copies(weight, wbuf, wsems)
    for copy in copies[:AHEAD]:
        copy.start()
    arrived = arrived.get()
    labels = arrived[pl.ds(SLOTS, tiles, stride=SLOTS + 1), :]
    label_out[...] = labels
    names = named_blocks(labels, 0, groups)
    field = slot_rows(arrived, 0, SLOTS // 2, tiles)
    cover = slot_rows(arrived, SLOTS // 2, SLOTS // 2, tiles)
    received, coverage = collected((field, cover), names)
    surface.wait()
    factor = mixing.get()[pl.ds(0, groups, stride=8), :]
    flux = factor * (coverage * values[...] - received)
    flux_out[...] = flux
    sums = products(flux, None, copies, wbuf, lhs, res)
    even, odd = dispatched(place.get(), entry_values(sums))
    half = low_half((tiles, LANES))
    pitch = out.shape[0] // tiles
    for i in range(SLOTS // 2):
        a, b = even[i * tiles : (i + 1) * tiles], odd[i * tiles : (i + 1) * tiles]
        out[pl.ds(i, tiles, stride=pitch), :] = jnp.where(half, a, b)


def solve_kernel(with_flux, p0, p1, p2, p3, mixing, extra, lev, *refs):
    if with_flux:
        out, buf, sems = refs
    else:
        out, unit_out, buf, sems = refs
    groups = extra.shape[0]
    chunk = 16
    levels = 8
    copies = []
    for d, part in enumerate((p0, p1, p2, p3)):
        source = lax.rem(lev[0] + 4 - d, 4)
        copies.append(
            pltpu.make_async_copy(
                part.at[pl.ds(0, 2 * groups)], buf.at[source], sems.at[d]
            )
        )
    for copy in copies:
        copy.start()
    kbuf, ebuf = mixing.get(), extra.get()
    for copy in copies:
        copy.wait()

    def body(step, carry):
        at = pl.multiple_of(step * chunk, chunk)
        rows = pl.ds(at, chunk)
        k = [
            kbuf[pl.ds(at * levels + level, chunk, stride=levels), :] for level in range(levels)
        ]
        cs, ds, es = [], [], []
        for level in range(levels):
            r = buf[level // 2, pl.ds((level % 2) * groups + at, chunk), :]
            if level == 0:
                inverse = 1.0 / (1.0 + k[1])
                if with_flux:
                    r = r - ebuf[rows, :]
                else:
                    es.append(k[0] * ebuf[rows, :] * inverse)
                ds.append(r * inverse)
            else:
                total = 1.0 + k[level] - k[level] * cs[-1]
                if level + 1 < levels:
                    total = total + k[level + 1]
                inverse = 1.0 / total
                ds.append((r + k[level] * ds[-1]) * inverse)
                if not with_flux:
                    es.append(k[level] * es[-1] * inverse)
            if level + 1 < levels:
                cs.append(k[level + 1] * inverse)
        for terms, ref in ((ds, out),) if with_flux else ((ds, out), (es, unit_out)):
            x = terms[-1]
            ref[pl.ds(at * levels + levels - 1, chunk, stride=levels), :] = x
            for level in range(levels - 2, -1, -1):
                x = terms[level] + cs[level] * x
                ref[pl.ds(at * levels + level, chunk, stride=levels), :] = x
        return carry

    lax.fori_loop(0, groups // chunk, body, 0)


def last_kernel(arrived, labels, base, unit, out, gain):
    tiles = labels.shape[0]
    arrived = arrived.get()
    groups = gain.shape[0]
    names = named_blocks(labels.get()[...], SLOTS, groups)
    (total,) = collected((slot_rows(arrived, 0, SLOTS // 2, tiles),), names)
    gain[...] = total
    bbuf, ubuf = base.get(), unit.get()

    def body(step, carry):
        at = pl.ds(pl.multiple_of(step * 8, 8), 8)
        out[at, :] = bbuf[at, :] + ubuf[at, :] * gain[pl.ds(step, 1), :]
        return carry

    lax.fori_loop(0, groups, body, 0, unroll=8)


VMEM = pl.BlockSpec(memory_space=pltpu.VMEM)
SMEM = pl.BlockSpec(memory_space=pltpu.SMEM)
HBM = pl.BlockSpec(memory_space=pltpu.HBM)
DMA = pltpu.SemaphoreType.DMA


def call(kernel, shapes, args, spaces, scratch=(), name=None, us=1.0, after=()):
    fetched = [i for i, space in enumerate(spaces) if space == "f"]
    outs = len(shapes) if isinstance(shapes, tuple) else 1

    def body(*refs):
        refs = list(refs)
        del refs[len(args) : len(args) + len(after)]
        end = len(refs) - 2 * len(fetched)
        for n, i in enumerate(fetched):
            refs[i] = Fetched(refs[i], refs[end + n], refs[end + len(fetched) + n])
        kernel(*refs[:end])

    extra = [pltpu.VMEM(args[i].shape, args[i].dtype) for i in fetched]
    extra += [DMA(()) for i in fetched]
    return pl.pallas_call(
        body,
        out_shape=shapes,
        in_specs=[{"v": VMEM, "s": SMEM, "h": HBM, "f": HBM}[space] for space in spaces]
        + [HBM] * len(after),
        out_specs=jax.tree.map(lambda _: VMEM, shapes),
        scratch_shapes=list(scratch) + extra,
        compiler_params=pltpu.CompilerParams(vmem_limit_bytes=64 * 1024 * 1024),
        cost_estimate=pl.CostEstimate(
            flops=0, bytes_accessed=int(us * 3.6e6), transcendentals=0
        ),
        name=name,
    )(*args, *after)


def shape(*dims, dtype=F32):
    return jax.ShapeDtypeStruct(dims, dtype)


def tile_rows(x, lead):
    levels, cells = x.shape[-2:]
    x = x.reshape(lead, levels, cells // LANES, LANES)
    return x.transpose(0, 2, 1, 3).reshape(lead * levels * cells // LANES, LANES)


def weight_rows(w):
    blocks, fan, size = w.shape
    w = w.reshape(blocks, fan, size // LANES, LANES).transpose(0, 2, 1, 3)
    return w.reshape(blocks * fan * size // LANES, LANES)


def on_device(
    air_state,
    sea_state,
    air_courant,
    sea_courant,
    air_mixing,
    sea_mixing,
    upward_weight,
    upward_target,
    upward_block,
    downward_weight,
    downward_target,
    downward_block,
    sea_mask,
):
    fields, pair, cells = air_state.shape
    tiles = lax.axis_size("tiles")
    levs = lax.axis_size("lev")
    rows = cells // LANES
    groups = sea_mask.shape[0] // 2
    lev = lax.axis_index("lev").astype(jnp.int32)
    tile = lax.axis_index("tiles").astype(jnp.int32)
    lev_ref = (lev + levs * (tile % 2)).reshape(1)
    states = (
        tile_rows(sea_state, fields),
        tile_rows(air_state, fields),
        tile_rows(sea_courant, 1),
        tile_rows(air_courant, 1),
    )
    size = pair * rows

    to_pair, to_other = call(
        edge_kernel,
        (shape(20, LANES),) * 2,
        (*states, lev_ref),
        "hhhhs",
        scratch=[
            pltpu.VMEM((2, fields + 1, 8, LANES), F32),
            pltpu.VMEM((2, fields + 1, 8, LANES), F32),
            DMA((2, fields + 1, 2)),
        ],
        name="edges",
        us=1.5,
    )
    pairs = [(i, i + 1 - 2 * (i % 2)) for i in range(tiles)]
    others = [(i, (i - 1 + 2 * (i % 2)) % tiles) for i in range(tiles)]
    ends = (
        lax.ppermute(to_pair, "tiles", pairs),
        lax.ppermute(to_other, "tiles", others),
    )
    extended = pltpu.VMEM((rows + 16, LANES), F32)

    def around(parts):
        return [parts[0]] + [
            lax.ppermute(parts[d], "lev", [(i, (i + d) % levs) for i in range(levs)])
            for d in range(1, levs)
        ]

    surface = call(
        surface_kernel,
        (shape(rows, LANES),) * 4,
        (states[0], states[2], *ends, lev_ref),
        "hfffs",
        scratch=[pltpu.VMEM((4, size, LANES), F32), extended, extended, DMA((4,))],
        name="surface",
        us=2.5,
    )
    surface_parts = around(surface)

    entries = 4 * groups
    place_up, place_down, labels, mask = call(
        functools.partial(prepare_kernel, tiles),
        (
            shape(2, entries, dtype=jnp.int32),
            shape(2, entries, dtype=jnp.int32),
            shape(tiles, LANES),
            shape(groups, LANES),
        ),
        (
            upward_target.T,
            upward_block.T,
            downward_target.T,
            downward_block.T,
            sea_mask.reshape(1, -1),
        ),
        "fffff",
        name="prepare",
        us=2.5,
        after=(surface[0],),
    )
    air_k = tile_rows(air_mixing, 1)
    sea_k = tile_rows(sea_mixing, 1)
    up_rows = weight_rows(upward_weight)
    down_rows = weight_rows(downward_weight)

    def workspace(count):
        return [
            pltpu.VMEM(up_rows.shape, BF16),
            pltpu.VMEM((groups * count, LANES), F32),
            pltpu.VMEM((groups * count, LANES), F32),
        ]

    pitch = SLOTS + 1
    outgoing = call(
        up_kernel,
        shape(tiles * pitch, LANES),
        (*surface_parts, mask, place_up, labels, up_rows, lev_ref),
        "hhhhfffhs",
        scratch=[pltpu.VMEM((rows, LANES), F32), *workspace(16), DMA(()), DMA((PIECES,))],
        name="upward",
        us=8.0,
    )

    def over_tiles(x):
        pitch = x.shape[0] // tiles
        y = x.reshape((tiles, pitch, LANES) if pitch % 8 == 0 else (tiles, 1, pitch * LANES))
        y = lax.all_to_all(y, "tiles", split_axis=0, concat_axis=0, tiled=True)
        return y.reshape(x.shape)

    def advected(state, courant, base, name):
        return call(
            functools.partial(advect_kernel, fields, base),
            tuple(shape(size, LANES) for _ in range(4)),
            (state, courant, *ends, lev_ref),
            "ffffs",
            scratch=[pltpu.VMEM((20, LANES), F32)] * 2 + [extended, extended],
            name=name,
            us=2.5,
            after=(outgoing,),
        )

    air = around(advected(states[1], states[3], 10, "advect_air"))
    sea_own = advected(states[0], states[2], 0, "advect_sea")
    arrived = over_tiles(outgoing)
    flux, returning, labels_down = call(
        middle_kernel,
        (shape(groups, LANES), shape(tiles * SLOTS // 2, LANES), shape(tiles, LANES)),
        (arrived, *air, air_k, place_down, down_rows, lev_ref),
        "fhhhhffhs",
        scratch=[pltpu.VMEM((rows, LANES), F32), *workspace(8), DMA(()), DMA((PIECES,))],
        name="middle",
        us=8.0,
        after=(sea_own[0],),
    )
    gained = over_tiles(returning)
    sea = around(sea_own)

    column = shape(8 * rows, LANES)

    def solve(with_flux, parts, k, extra, name, after=()):
        return call(
            functools.partial(solve_kernel, with_flux),
            column if with_flux else (column, column),
            (*parts, k, extra, lev_ref),
            "hhhhffs",
            scratch=[pltpu.VMEM((4, size, LANES), F32), DMA((4,))],
            name=name,
            us=3.0,
            after=after,
        )

    air_out = solve(True, air, air_k, flux, "solve_air")
    base, unit = solve(False, sea, sea_k, mask, "solve_sea", (air_out,))
    sea_out = call(
        last_kernel,
        column,
        (gained, labels_down, base, unit),
        "ffff",
        scratch=[pltpu.VMEM((rows, LANES), F32)],
        name="last",
        us=2.0,
    )

    def levels_first(x):
        return x.reshape(rows, 8, LANES).transpose(1, 0, 2).reshape(1, 8, cells)

    return levels_first(air_out), levels_first(sea_out)


def solution(mesh):
    return jax.shard_map(
        on_device,
        mesh=mesh,
        in_specs=(
            P(None, "lev", "tiles"),
            P(None, "lev", "tiles"),
            P("lev", "tiles"),
            P("lev", "tiles"),
            P(None, "tiles"),
            P(None, "tiles"),
            P("tiles", None, None),
            P("tiles", None),
            P("tiles", None),
            P("tiles", None, None),
            P("tiles", None),
            P("tiles", None),
            P("tiles"),
        ),
        out_specs=(P("lev", None, "tiles"), P("lev", None, "tiles")),
        check_vma=False,
    )
```

```python
import functools

import jax
import jax.numpy as jnp
from jax import lax
from jax.experimental import pallas as pl
from jax.experimental.pallas import tpu as pltpu
from jax.sharding import PartitionSpec as P

BLOCK = 64
LANES = 128
SLOTS = 16
PIECES = 4
AHEAD = 2
F32 = jnp.float32
BF16 = jnp.bfloat16
NT = (((1,), (1,)), ((), ()))
NN = (((1,), (0,)), ((), ()))


def dot(a, b, dims=NN):
    return lax.dot_general(a, b, dims, preferred_element_type=F32)


def split(x):
    high = x.astype(BF16)
    return high, (x - high.astype(F32)).astype(BF16)


def iota(shape, dim):
    return lax.broadcasted_iota(jnp.int32, shape, dim)


def low_half(shape):
    return iota(shape, len(shape) - 1) < BLOCK


def swap(x):
    return pltpu.roll(x, BLOCK, x.ndim - 1)


class Fetched:
    def __init__(self, source, buf, sem):
        self.copy = pltpu.make_async_copy(source, buf, sem)
        self.shape = source.shape
        self.buf = buf
        self.waiting = True
        self.copy.start()

    def get(self):
        if self.waiting:
            self.copy.wait()
            self.waiting = False
        return self.buf


def onehot(condition):
    return jnp.where(condition, 1.0, 0.0).astype(BF16)


def prepare_kernel(
    tiles, ut, ub, dt, db, mask, up_out, down_out, label_out, mask_out, ready_out
):
    blocks = ut.shape[1]
    groups = blocks // 2
    entries = 2 * blocks
    source, lane = iota((blocks, blocks), 0), iota((blocks, blocks), 1)
    turn = onehot(source == 2 * (lane & (groups - 1)) + lane // groups)
    lists = [x.get()[...] for x in (ut, ub, dt, db, mask)]
    stacked = jnp.concatenate([x.astype(F32) for x in lists], 0)
    stacked = jnp.concatenate([stacked, jnp.zeros((16 - stacked.shape[0], blocks), F32)], 0)
    stacked = dot(stacked.astype(BF16), turn)

    def entry_row(at):
        pair = stacked[at : at + 2]
        parts = [
            pair[k : k + 1, odd * groups : (odd + 1) * groups]
            for odd in range(2)
            for k in range(2)
        ]
        return jnp.concatenate(parts, 1)

    tile_row = iota((tiles, entries), 0).astype(F32)
    earlier = onehot(iota((entries, entries), 0) < iota((entries, entries), 1))
    labels = None
    for first, out, base in ((0, up_out, 0), (4, down_out, SLOTS)):
        target, block = entry_row(first), entry_row(first + 2)
        named = jnp.where(target == tile_row, 1.0, 0.0)
        rank = jnp.sum(named * dot(named.astype(BF16), earlier), 0, keepdims=True)
        rank = rank.astype(jnp.int32)
        target = target.astype(jnp.int32)
        at = (rank // 2) * tiles + target
        for half in range(2):
            out[half : half + 1, :] = jnp.where((rank & 1) == half, at, -1)
        carried = (named * (block + 1.0)).astype(BF16)
        chosen = onehot(iota((LANES, entries), 0) == rank + base)
        term = dot(carried, chosen, NT)
        labels = term if labels is None else labels + term
    label_out[...] = labels
    diagonal = iota((groups, groups), 0) == iota((groups, groups), 1)
    spread = None
    for odd in range(2):
        row = stacked[8:9, odd * groups : (odd + 1) * groups]
        picked = jnp.where(diagonal, row, 0.0).astype(BF16)
        side = onehot((iota((groups, LANES), 1) // BLOCK) == odd)
        term = dot(picked, side)
        spread = term if spread is None else spread + term
    mask_out[...] = spread
    ready_out[...] = spread[0:8]


def edge_kernel(sea, air, sea_c, air_c, place, pair_out, next_out, first, last, sems):
    fields = 4
    copies = []
    for n, (state, courant) in enumerate(((sea, sea_c), (air, air_c))):
        size = courant.shape[0]
        for at in range(fields + 1):
            source, base = (state, at * size) if at < fields else (courant, 0)
            for side, (buf, start) in enumerate(((first, 0), (last, size - 8))):
                copies.append(
                    pltpu.make_async_copy(
                        source.at[pl.ds(base + start, 8)], buf.at[n, at], sems.at[n, at, side]
                    )
                )
    for copy in copies:
        copy.start()
    for copy in copies:
        copy.wait()
    for n in range(2):
        for at in range(fields + 1):
            row = n * 2 * (fields + 1) + 2 * at
            low, high = first[n, at, 0:2, :], last[n, at, 6:8, :]
            pair_out[row : row + 2, :] = jnp.where(place[0] // 4 == 0, high, low)
            next_out[row : row + 2, :] = jnp.where(place[0] // 4 == 0, low, high)


def neighbours(pair, other, place):
    pair, other = pair.get()[...], other.get()[...]
    even = place[0] // 4 == 0
    return jnp.where(even, other, pair), jnp.where(even, pair, other)


def stepped(x, low, high, positive, negative, buf):
    rows = x.shape[0]
    total = buf.shape[0]
    lane = iota((total, LANES), 1)
    first = lane == 0
    last = lane == LANES - 1
    buf[0:8, :] = jnp.broadcast_to(low, (8, LANES))
    buf[8 : rows + 8, :] = x
    buf[rows + 8 :, :] = jnp.broadcast_to(high, (8, LANES))
    x = buf[...]
    for step in range(2):
        below = pltpu.roll(x, 1, 1)
        below = jnp.where(first, pltpu.roll(below, 1, 0), below)
        above = pltpu.roll(x, LANES - 1, 1)
        above = jnp.where(last, pltpu.roll(above, total - 1, 0), above)
        x = x - positive * (x - below) - negative * (above - x)
    return x[8 : rows + 8, :]


def speeds(c, low, high, buf):
    rows = c.shape[0]
    buf[0:8, :] = jnp.broadcast_to(low, (8, LANES))
    buf[8 : rows + 8, :] = c
    buf[rows + 8 :, :] = jnp.broadcast_to(high, (8, LANES))
    c = buf[...]
    return jnp.maximum(c, 0.0), jnp.minimum(c, 0.0)


def upwind(x, positive, negative, below, above):
    return x - positive * (x - below) - negative * (above - x)


def sea_kernel(fields, state, courant, place, o0, o1, o2, o3, sbuf, sems):
    rows = courant.shape[0] // 2
    size = 2 * rows
    outs = (o0, o1, o2, o3)
    order = (1, 2, 3, 0)

    def copy(d):
        field = lax.rem(place[0] + d, fields)
        at = pl.multiple_of(field * size, size)
        return pltpu.make_async_copy(state.at[pl.ds(at, size)], sbuf.at[d], sems.at[d])

    for d in order:
        copy(d).start()
    lane = iota((rows, LANES), 1)
    first = lane == 0
    last = lane == LANES - 1
    courant = courant.get()
    signs = []
    for level in range(2):
        c = courant[pl.ds(level, rows, stride=2), :]
        signs.append((jnp.maximum(c, 0.0), jnp.minimum(c, 0.0)))
    for d in order:
        copy(d).wait()
        out = outs[d]
        for level in range(2):
            positive, negative = signs[level]
            x = sbuf[d, pl.ds(level, rows, stride=2), :]
            for step in range(2):
                below = pltpu.roll(x, 1, 1)
                below = jnp.where(first, pltpu.roll(below, 1, 0), below)
                above = pltpu.roll(x, LANES - 1, 1)
                above = jnp.where(last, pltpu.roll(above, rows - 1, 0), above)
                x = upwind(x, positive, negative, below, above)
            out[level * rows : (level + 1) * rows, :] = x
        out[size : size + 2, :] = sbuf[d, 0:2, :]
        out[size + 2 : size + 4, :] = sbuf[d, size - 2 : size, :]
        out[size + 4 : size + 6, :] = courant[0:2, :]
        out[size + 6 : size + 8, :] = courant[size - 2 : size, :]


def mended(first, last, left, right):
    low = low_half(first[0].shape)
    out = []
    for inner, outer, kept in ((first, left, low), (last, right, jnp.logical_not(low))):
        x = jnp.where(kept, inner[0], outer[0])
        c = jnp.where(kept, inner[1], outer[1])
        positive, negative = jnp.maximum(c, 0.0), jnp.minimum(c, 0.0)
        for step in range(2):
            x = upwind(x, positive, negative, pltpu.roll(x, 1, 1), pltpu.roll(x, LANES - 1, 1))
        out.append(x)
    return out


def mend(row, mended_row, at_end):
    lane = iota(row.shape, 1)
    return jnp.where(lane >= LANES - 2 if at_end else lane < 2, mended_row, row)


def outer_rows(halo, field, level, place):
    rows = (halo.shape[0] - 8) // 2
    pair, other = [
        (halo[pl.ds(n * rows + 2 * field + level, 1), :], halo[n * rows + 8 + level : n * rows + 9 + level, :])
        for n in range(2)
    ]
    even = place[0] // 4 == 0
    left = [jnp.where(even, b, a) for a, b in zip(pair, other)]
    right = [jnp.where(even, a, b) for a, b in zip(pair, other)]
    return left, right


def advect_kernel(
    fields, base, state, courant, mixing, pair, other, lev,
    o0, o1, o2, o3, factor_out, lows, highs, xbuf, cbuf,
):
    rows = courant.shape[0] // 2
    factor_out[...] = mixing.get()[pl.ds(0, rows, stride=8), :]
    lows[...], highs[...] = neighbours(pair, other, lev)
    for level in range(2):
        c = courant.get()[pl.ds(level, rows, stride=2), :]
        at = base + 8 + level
        positive, negative = speeds(c, lows[at : at + 1, :], highs[at : at + 1, :], cbuf)
        for d, out in enumerate((o0, o1, o2, o3)):
            field = lax.rem(lev[0] + d, fields)
            x = state.get()[pl.ds(field * 2 * rows + level, rows, stride=2), :]
            at = pl.ds(base + 2 * field + level, 1)
            x = stepped(x, lows[at, :], highs[at, :], positive, negative, xbuf)
            out[level * rows : (level + 1) * rows, :] = x


def weight_copies(weight, wbuf, sems):
    pieces = sems.shape[0]
    size = weight.shape[0] // pieces
    return [
        pltpu.make_async_copy(
            weight.at[pl.ds(n * size, size)], wbuf.at[pl.ds(n * size, size)], sems.at[n]
        )
        for n in range(pieces)
    ]


def product_rows(values, ones, put):
    half = low_half(values.shape)
    zero = jnp.zeros(values.shape, F32)
    high = values.astype(BF16).astype(F32)
    sets = [(0, 2, high), (2, 2, values - high)]
    if ones is not None:
        sets.append((8, 0, ones))
    for base, gap, x in sets:
        turned = swap(x)
        for odd in range(2):
            for parity in range(2):
                row = base + odd * (2 + gap) + parity
                chosen = turned if odd != parity else x
                put(row, jnp.where(half == (parity == 0), chosen, zero))
    if ones is not None:
        for row in range(12, 16):
            put(row, zero)


def product_sums(got, with_ones):
    half = low_half(got(0).shape)
    out = [jnp.where(half, got(p) + got(2 + p), got(4 + p) + got(6 + p)) for p in range(2)]
    if with_ones:
        out.extend(jnp.where(half, got(8 + p), got(10 + p)) for p in range(2))
    return out


def products(values, ones, copies, wbuf, lhs, res):
    groups = values.shape[0]
    count = 8 if ones is None else 16

    def put(row, x):
        lhs[pl.ds(row, groups, stride=count), :] = x

    product_rows(values, ones, put)

    def body(step, carry):
        w = wbuf[pl.ds(pl.multiple_of(step * 2 * LANES, 2 * LANES), 2 * LANES), :]
        both = pl.ds(pl.multiple_of(step * 2 * count, 2 * count), 2 * count)
        out = dot(lhs[both, :].astype(BF16), w, NT)
        for n in range(2):
            at = pl.ds(pl.multiple_of((2 * step + n) * count, count), count)
            res[at, :] = out[n * count : (n + 1) * count, n * LANES : (n + 1) * LANES]
        return carry

    each = groups // 2 // len(copies)
    for n, copy in enumerate(copies):
        copy.wait()
        if n + AHEAD + 1 < len(copies):
            copies[n + AHEAD + 1].start()
        lax.fori_loop(n * each, (n + 1) * each, body, 0, unroll=each)
    return product_sums(lambda row: res[pl.ds(row, groups, stride=count), :], ones is not None)


def entry_order():
    row, column = iota((256, 512), 0), iota((256, 512), 1)
    same = ((row >> 6) & 1) * 2 + (row & 1) == (column >> 7)
    cell = ((row >> 1) & 31) * 2 + (row >> 7)
    return onehot(same & (cell == (column & 63)))


def entry_values(sums, order):
    def ordered(pair):
        high, low = split(jnp.concatenate(pair, 1))
        return dot(high, order), dot(low, order)

    y = ordered(sums[:2])
    if len(sums) > 2:
        half = low_half(y[0].shape[:1] + (LANES,))
        half = jnp.concatenate([half] * 4, 1)
        y = [jnp.where(half, a, b) for a, b in zip(y, ordered(sums[2:]))]
    terms = []
    for part in y:
        part = part.astype(BF16)
        terms.append(jnp.concatenate([part[:, q * LANES : (q + 1) * LANES] for q in range(4)], 0))
    return jnp.concatenate(terms, 1)


def slot_order(place):
    count = place.shape[1]
    return [onehot(iota((count, count), 0) == place[half : half + 1, :]) for half in range(2)]


def dispatched(orders, entries):
    out = []
    for order in orders:
        slots = dot(order, entries)
        out.append(slots[:, :LANES] + slots[:, LANES:])
    return out


def surface_copy(parts, at, lev, buf, sem):
    copies = [
        pltpu.make_async_copy(part.at[pl.ds(at, buf.shape[0])], buf, sem) for part in parts
    ]
    for d, copy in enumerate(copies):

        @pl.when(lev[0] % 4 == d)
        def start(copy=copy):
            copy.start()

    return copies[0]


def up_kernel(
    p0, p1, p2, p3, h0, h1, h2, h3, mask, place, labels, weight, lev,
    out, values, halo, wbuf, lhs, res, sems, wsems,
):
    tiles = labels.shape[0]
    rows = mask.shape[0]
    own = surface_copy((h0, h1, h2, h3), 0, lev, halo, sems.at[1])
    field = surface_copy((p0, p1, p2, p3), 0, lev, values, sems.at[0])
    copies = weight_copies(weight, wbuf, wsems)
    for copy in copies[:AHEAD]:
        copy.start()
    order = entry_order()
    slots = slot_order(place.get())
    field.wait()
    own.wait()
    copies[AHEAD].start()
    ends = values[2 * rows :, :]
    mended_rows = mended(
        (ends[0:1], ends[4:5]), (ends[2:3], ends[6:7]), *outer_rows(halo, lev[0] % 4, 0, lev)
    )
    for n, at in enumerate((0, rows - 1)):
        values[at : at + 1, :] = mend(values[at : at + 1, :], mended_rows[n], n == 1)
    mask_value = mask.get()[...]
    sums = products(values[0:rows, :] * mask_value, mask_value, copies, wbuf, lhs, res)
    even, odd = dispatched(slots, entry_values(sums, order))
    half = low_half((tiles, LANES))
    pitch = out.shape[0] // tiles
    for i in range(SLOTS // 2):
        a, b = even[i * tiles : (i + 1) * tiles], odd[i * tiles : (i + 1) * tiles]
        out[pl.ds(i, tiles, stride=pitch), :] = jnp.where(half, a, swap(b))
        out[pl.ds(SLOTS // 2 + i, tiles, stride=pitch), :] = jnp.where(half, swap(a), b)
    out[pl.ds(SLOTS, tiles, stride=pitch), :] = labels.get()[...]


def named_blocks(labels, base, blocks):
    turned = jnp.transpose(jnp.concatenate([labels, labels], 0))
    half = low_half((1, LANES))
    out = []
    for slot_half in range(2):
        row = []
        for i in range(0, SLOTS // 2, 2):
            at = base + 2 * i + slot_half
            row.append(jnp.where(half, turned[at : at + 1], turned[at + 2 : at + 3]))
        row = jnp.concatenate(row, 1).astype(jnp.int32)
        for odd in range(2):
            out.append(onehot(2 * iota((blocks, row.shape[1]), 0) + odd + 1 == row))
    return out


def collected(parts, names):
    halves = []
    for part in parts:
        halves.extend(split(part))
    values = jnp.concatenate(halves, 1)
    sums = [dot(name, values) for name in names]
    half = low_half((sums[0].shape[0], LANES))
    out = []
    for n in range(len(parts)):
        at = 2 * n * LANES
        g = [s[:, at : at + LANES] + s[:, at + LANES : at + 2 * LANES] for s in sums]
        out.append(jnp.where(half, g[0] + swap(g[2]), swap(g[1]) + g[3]))
    return out


def slot_rows(arrived, start, count, tiles):
    pitch = arrived.shape[0] // tiles
    return jnp.concatenate(
        [arrived[pl.ds(start + i, tiles, stride=pitch), :] for i in range(count)], 0
    )


def middle_kernel(
    arrived, p0, p1, p2, p3, factor, place, weight, lev,
    flux_out, out, label_out, values, wbuf, lhs, res, sem, wsems,
):
    groups = flux_out.shape[0]
    tiles = label_out.shape[0]
    surface = surface_copy((p0, p1, p2, p3), 0, lev, values, sem)
    copies = weight_copies(weight, wbuf, wsems)
    for copy in copies[:AHEAD]:
        copy.start()
    order = entry_order()
    slots = slot_order(place.get())
    arrived = arrived.get()
    copies[AHEAD].start()
    labels = arrived[pl.ds(SLOTS, tiles, stride=SLOTS + 1), :]
    label_out[...] = labels
    names = named_blocks(labels, 0, groups)
    field = slot_rows(arrived, 0, SLOTS // 2, tiles)
    cover = slot_rows(arrived, SLOTS // 2, SLOTS // 2, tiles)
    received, coverage = collected((field, cover), names)
    surface.wait()
    flux = factor.get()[...] * (coverage * values[...] - received)
    flux_out[...] = flux
    sums = products(flux, None, copies, wbuf, lhs, res)
    even, odd = dispatched(slots, entry_values(sums, order))
    half = low_half((tiles, LANES))
    pitch = out.shape[0] // tiles
    for i in range(SLOTS // 2):
        a, b = even[i * tiles : (i + 1) * tiles], odd[i * tiles : (i + 1) * tiles]
        out[pl.ds(i, tiles, stride=pitch), :] = jnp.where(half, a, b)


def solve_kernel(with_flux, p0, p1, p2, p3, *refs):
    if with_flux:
        mixing, extra, lev, out, buf, sems = refs
        sources = [((p0, p1, p2, p3), buf, 0)]
    else:
        h0, h1, h2, h3, mixing, extra, lev, out, unit_out, buf, halo, sems = refs
        sources = [((p0, p1, p2, p3), buf, 0), ((h0, h1, h2, h3), halo, 4)]
    groups = extra.shape[0]
    chunk = 16
    levels = 8
    copies = []
    for parts, to, base in sources:
        for d, part in enumerate(parts):
            source = lax.rem(lev[0] + 4 - d, 4)
            copies.append(pltpu.make_async_copy(part, to.at[source], sems.at[base + d]))
    for copy in copies:
        copy.start()
    kbuf, ebuf = mixing.get(), extra.get()
    for copy in copies:
        copy.wait()
    if not with_flux:
        parts = [[[], []] for n in range(4)]
        for level in range(levels):
            at = 2 * groups + level % 2
            ends = [buf[level // 2, at + 2 * n : at + 2 * n + 1, :] for n in range(4)]
            left, right = outer_rows(halo.at[level // 2], lev[0] % 4, level % 2, lev)
            for n, rows in enumerate(((ends[0], ends[2]), (ends[1], ends[3]), left, right)):
                parts[n][0].append(rows[0])
                parts[n][1].append(rows[1])
        mended_rows = mended(*[[jnp.concatenate(rows, 0) for rows in part] for part in parts])
        for level in range(levels):
            at = (level % 2) * groups
            for n, row in enumerate((at, at + groups - 1)):
                old = buf[level // 2, row : row + 1, :]
                new = mended_rows[n][level : level + 1]
                buf[level // 2, row : row + 1, :] = mend(old, new, n == 1)

    def body(step, carry):
        at = pl.multiple_of(step * chunk, chunk)
        rows = pl.ds(at, chunk)
        k = [
            kbuf[pl.ds(at * levels + level, chunk, stride=levels), :] for level in range(levels)
        ]
        cs, ds, es = [], [], []
        for level in range(levels):
            r = buf[level // 2, pl.ds((level % 2) * groups + at, chunk), :]
            if level == 0:
                inverse = 1.0 / (1.0 + k[1])
                if with_flux:
                    r = r - ebuf[rows, :]
                else:
                    es.append(k[0] * ebuf[rows, :] * inverse)
                ds.append(r * inverse)
            else:
                total = 1.0 + k[level] - k[level] * cs[-1]
                if level + 1 < levels:
                    total = total + k[level + 1]
                inverse = 1.0 / total
                ds.append((r + k[level] * ds[-1]) * inverse)
                if not with_flux:
                    es.append(k[level] * es[-1] * inverse)
            if level + 1 < levels:
                cs.append(k[level + 1] * inverse)
        for terms, ref in ((ds, out),) if with_flux else ((ds, out), (es, unit_out)):
            x = terms[-1]
            ref[pl.ds(at * levels + levels - 1, chunk, stride=levels), :] = x
            for level in range(levels - 2, -1, -1):
                x = terms[level] + cs[level] * x
                ref[pl.ds(at * levels + level, chunk, stride=levels), :] = x
        return carry

    lax.fori_loop(0, groups // chunk, body, 0)


def last_kernel(arrived, labels, base, unit, out, gain, obuf, sems):
    tiles = labels.shape[0]
    groups = gain.shape[0]
    names = named_blocks(labels.get()[...], SLOTS, groups)
    (total,) = collected((slot_rows(arrived.get(), 0, SLOTS // 2, tiles),), names)
    gain[...] = total
    bbuf, ubuf = base.get(), unit.get()

    def body(step, carry):
        at = pl.ds(pl.multiple_of(step * 8, 8), 8)
        obuf[at, :] = bbuf[at, :] + ubuf[at, :] * gain[pl.ds(step, 1), :]
        return carry

    pieces = sems.shape[0]
    copies = []
    for n in range(pieces):
        lax.fori_loop(n * groups // pieces, (n + 1) * groups // pieces, body, 0, unroll=8)
        rows = pl.ds(n * 8 * groups // pieces, 8 * groups // pieces)
        copies.append(pltpu.make_async_copy(obuf.at[rows], out.at[rows], sems.at[n]))
        copies[n].start()
    for copy in copies:
        copy.wait()


VMEM = pl.BlockSpec(memory_space=pltpu.VMEM)
SMEM = pl.BlockSpec(memory_space=pltpu.SMEM)
HBM = pl.BlockSpec(memory_space=pltpu.HBM)
DMA = pltpu.SemaphoreType.DMA


def call(kernel, shapes, args, spaces, scratch=(), name=None, us=1.0, after=(), to=None):
    fetched = [i for i, space in enumerate(spaces) if space == "f"]
    outs = len(shapes) if isinstance(shapes, tuple) else 1

    def body(*refs):
        refs = list(refs)
        del refs[len(args) : len(args) + len(after)]
        end = len(refs) - 2 * len(fetched)
        for n, i in enumerate(fetched):
            refs[i] = Fetched(refs[i], refs[end + n], refs[end + len(fetched) + n])
        kernel(*refs[:end])

    extra = [pltpu.VMEM(args[i].shape, args[i].dtype) for i in fetched]
    extra += [DMA(()) for i in fetched]
    return pl.pallas_call(
        body,
        out_shape=shapes,
        in_specs=[{"v": VMEM, "s": SMEM, "h": HBM, "f": HBM}[space] for space in spaces]
        + [HBM] * len(after),
        out_specs=jax.tree.map(lambda _: VMEM, shapes) if to is None else to,
        scratch_shapes=list(scratch) + extra,
        compiler_params=pltpu.CompilerParams(vmem_limit_bytes=64 * 1024 * 1024),
        cost_estimate=pl.CostEstimate(
            flops=0, bytes_accessed=int(us * 3.6e6), transcendentals=0
        ),
        name=name,
    )(*args, *after)


def shape(*dims, dtype=F32):
    return jax.ShapeDtypeStruct(dims, dtype)


def tile_rows(x, lead):
    levels, cells = x.shape[-2:]
    x = x.reshape(lead, levels, cells // LANES, LANES)
    return x.transpose(0, 2, 1, 3).reshape(lead * levels * cells // LANES, LANES)


def weight_rows(w):
    blocks, fan, size = w.shape
    w = w.reshape(blocks, fan, size // LANES, LANES).transpose(0, 2, 1, 3)
    return w.reshape(blocks * fan * size // LANES, LANES)


def on_device(
    air_state,
    sea_state,
    air_courant,
    sea_courant,
    air_mixing,
    sea_mixing,
    upward_weight,
    upward_target,
    upward_block,
    downward_weight,
    downward_target,
    downward_block,
    sea_mask,
):
    fields, pair, cells = air_state.shape
    tiles = lax.axis_size("tiles")
    levs = lax.axis_size("lev")
    rows = cells // LANES
    groups = sea_mask.shape[0] // 2
    lev = lax.axis_index("lev").astype(jnp.int32)
    tile = lax.axis_index("tiles").astype(jnp.int32)
    lev_ref = (lev + levs * (tile % 2)).reshape(1)
    states = (
        tile_rows(sea_state, fields),
        tile_rows(air_state, fields),
        tile_rows(sea_courant, 1),
        tile_rows(air_courant, 1),
    )
    size = pair * rows

    to_pair, to_other = call(
        edge_kernel,
        (shape(20, LANES),) * 2,
        (*states, lev_ref),
        "hhhhs",
        scratch=[
            pltpu.VMEM((2, fields + 1, 8, LANES), F32),
            pltpu.VMEM((2, fields + 1, 8, LANES), F32),
            DMA((2, fields + 1, 2)),
        ],
        name="edges",
        us=1.5,
    )
    pairs = [(i, i + 1 - 2 * (i % 2)) for i in range(tiles)]
    others = [(i, (i - 1 + 2 * (i % 2)) % tiles) for i in range(tiles)]
    ends = (
        lax.ppermute(to_pair, "tiles", pairs),
        lax.ppermute(to_other, "tiles", others),
    )
    extended = pltpu.VMEM((rows + 16, LANES), F32)

    def around(parts):
        return [parts[0]] + [
            lax.ppermute(parts[d], "lev", [(i, (i + d) % levs) for i in range(levs)])
            for d in range(1, levs)
        ]

    sea_own = call(
        functools.partial(sea_kernel, fields),
        (shape(size + 8, LANES),) * 4,
        (states[0], states[2], lev_ref),
        "hfs",
        scratch=[pltpu.VMEM((4, size, LANES), F32), DMA((4,))],
        name="sea",
        us=3.0,
        after=(to_pair,),
    )
    sea = around(sea_own)
    entries = 4 * groups
    place_up, place_down, labels, mask, ready = call(
        functools.partial(prepare_kernel, tiles),
        (
            shape(2, entries, dtype=jnp.int32),
            shape(2, entries, dtype=jnp.int32),
            shape(tiles, LANES),
            shape(groups, LANES),
            shape(8, LANES),
        ),
        (
            upward_target.T,
            upward_block.T,
            downward_target.T,
            downward_block.T,
            sea_mask.reshape(1, -1),
        ),
        "fffff",
        name="prepare",
        us=2.5,
        after=(sea_own[0],),
    )
    halo = around([jnp.concatenate([*ends, ready], 0)] * 4)
    air_k = tile_rows(air_mixing, 1)
    sea_k = tile_rows(sea_mixing, 1)
    up_rows = weight_rows(upward_weight)
    down_rows = weight_rows(downward_weight)

    def workspace(count):
        return [
            pltpu.VMEM(up_rows.shape, BF16),
            pltpu.VMEM((groups * count, LANES), F32),
            pltpu.VMEM((groups * count, LANES), F32),
        ]

    pitch = SLOTS + 1
    outgoing = call(
        up_kernel,
        shape(tiles * pitch, LANES),
        (*sea, *halo, mask, place_up, labels, up_rows, lev_ref),
        "hhhhhhhhfffhs",
        scratch=[
            pltpu.VMEM((size + 8, LANES), F32),
            pltpu.VMEM(halo[0].shape, F32),
            *workspace(16),
            DMA((2,)),
            DMA((PIECES,)),
        ],
        name="upward",
        us=8.0,
    )

    def over_tiles(x):
        pitch = x.shape[0] // tiles
        y = x.reshape((tiles, pitch, LANES) if pitch % 8 == 0 else (tiles, 1, pitch * LANES))
        y = lax.all_to_all(y, "tiles", split_axis=0, concat_axis=0, tiled=True)
        return y.reshape(x.shape)

    def advected(state, courant, base, name):
        return call(
            functools.partial(advect_kernel, fields, base),
            (shape(size, LANES),) * 4 + (shape(rows, LANES),),
            (state, courant, air_k, *ends, lev_ref),
            "fffffs",
            scratch=[pltpu.VMEM((20, LANES), F32)] * 2 + [extended, extended],
            name=name,
            us=2.5,
            after=(outgoing,),
        )

    *air, factor = advected(states[1], states[3], 10, "advect_air")
    air = around(air)
    arrived = over_tiles(outgoing)
    flux, returning, labels_down = call(
        middle_kernel,
        (shape(groups, LANES), shape(tiles * SLOTS // 2, LANES), shape(tiles, LANES)),
        (arrived, *air, factor, place_down, down_rows, lev_ref),
        "fhhhhffhs",
        scratch=[pltpu.VMEM((rows, LANES), F32), *workspace(8), DMA(()), DMA((PIECES,))],
        name="middle",
        us=8.0,
    )
    gained = over_tiles(returning)

    column = shape(8 * rows, LANES)

    def solve(with_flux, parts, k, extra, name):
        part, halo_part = (4, *parts[0].shape), (4, *halo[0].shape)
        return call(
            functools.partial(solve_kernel, with_flux),
            column if with_flux else (column, column),
            (*parts, k, extra, lev_ref),
            "h" * len(parts) + "ffs",
            scratch=[
                pltpu.VMEM(part, F32),
                *([] if with_flux else [pltpu.VMEM(halo_part, F32)]),
                DMA((len(parts),)),
            ],
            name=name,
            us=3.0,
        )

    base, unit = solve(False, [*sea, *halo], sea_k, mask, "solve_sea")
    air_out = solve(True, air, air_k, flux, "solve_air")
    sea_out = call(
        last_kernel,
        column,
        (gained, labels_down, base, unit),
        "ffff",
        scratch=[pltpu.VMEM((rows, LANES), F32), pltpu.VMEM((8 * rows, LANES), F32), DMA((4,))],
        name="last",
        to=HBM,
        us=2.0,
    )

    def levels_first(x):
        return x.reshape(rows, 8, LANES).transpose(1, 0, 2).reshape(1, 8, cells)

    return levels_first(air_out), levels_first(sea_out)


def solution(mesh):
    return jax.shard_map(
        on_device,
        mesh=mesh,
        in_specs=(
            P(None, "lev", "tiles"),
            P(None, "lev", "tiles"),
            P("lev", "tiles"),
            P("lev", "tiles"),
            P(None, "tiles"),
            P(None, "tiles"),
            P("tiles", None, None),
            P("tiles", None),
            P("tiles", None),
            P("tiles", None, None),
            P("tiles", None),
            P("tiles", None),
            P("tiles"),
        ),
        out_specs=(P("lev", None, "tiles"), P("lev", None, "tiles")),
        check_vma=False,
    )
```

```python
import functools

import jax
import jax.numpy as jnp
from jax import lax
from jax.experimental import pallas as pl
from jax.experimental.pallas import tpu as pltpu
from jax.sharding import PartitionSpec as P

BLOCK = 64
LANES = 128
SLOTS = 16
PIECES = 4
AHEAD = 2
F32 = jnp.float32
BF16 = jnp.bfloat16
NT = (((1,), (1,)), ((), ()))
NN = (((1,), (0,)), ((), ()))


def dot(a, b, dims=NN):
    return lax.dot_general(a, b, dims, preferred_element_type=F32)


def split(x):
    high = x.astype(BF16)
    return high, (x - high.astype(F32)).astype(BF16)


def iota(shape, dim):
    return lax.broadcasted_iota(jnp.int32, shape, dim)


def low_half(shape):
    return iota(shape, len(shape) - 1) < BLOCK


def swap(x):
    return pltpu.roll(x, BLOCK, x.ndim - 1)


class Fetched:
    def __init__(self, source, buf, sem):
        self.copy = pltpu.make_async_copy(source, buf, sem)
        self.shape = source.shape
        self.buf = buf
        self.waiting = True
        self.copy.start()

    def get(self):
        if self.waiting:
            self.copy.wait()
            self.waiting = False
        return self.buf


def onehot(condition):
    return jnp.where(condition, 1.0, 0.0).astype(BF16)


def prepare_kernel(
    tiles, ut, ub, dt, db, mask, up_out, down_out, label_out, mask_out, ready_out
):
    blocks = ut.shape[1]
    groups = blocks // 2
    entries = 2 * blocks
    source, lane = iota((blocks, blocks), 0), iota((blocks, blocks), 1)
    turn = onehot(source == 2 * (lane & (groups - 1)) + lane // groups)
    lists = [x.get()[...] for x in (ut, ub, dt, db, mask)]
    stacked = jnp.concatenate([x.astype(F32) for x in lists], 0)
    stacked = jnp.concatenate([stacked, jnp.zeros((16 - stacked.shape[0], blocks), F32)], 0)
    stacked = dot(stacked.astype(BF16), turn)

    def entry_row(at):
        pair = stacked[at : at + 2]
        parts = [
            pair[k : k + 1, odd * groups : (odd + 1) * groups]
            for odd in range(2)
            for k in range(2)
        ]
        return jnp.concatenate(parts, 1)

    tile_row = iota((tiles, entries), 0).astype(F32)
    earlier = onehot(iota((entries, entries), 0) < iota((entries, entries), 1))
    labels = None
    for first, out, base in ((0, up_out, 0), (4, down_out, SLOTS)):
        target, block = entry_row(first), entry_row(first + 2)
        named = jnp.where(target == tile_row, 1.0, 0.0)
        rank = jnp.sum(named * dot(named.astype(BF16), earlier), 0, keepdims=True)
        rank = rank.astype(jnp.int32)
        target = target.astype(jnp.int32)
        at = (rank // 2) * tiles + target
        for half in range(2):
            out[half : half + 1, :] = jnp.where((rank & 1) == half, at, -1)
        carried = (named * (block + 1.0)).astype(BF16)
        chosen = onehot(iota((LANES, entries), 0) == rank + base)
        term = dot(carried, chosen, NT)
        labels = term if labels is None else labels + term
    label_out[...] = labels
    diagonal = iota((groups, groups), 0) == iota((groups, groups), 1)
    spread = None
    for odd in range(2):
        row = stacked[8:9, odd * groups : (odd + 1) * groups]
        picked = jnp.where(diagonal, row, 0.0).astype(BF16)
        side = onehot((iota((groups, LANES), 1) // BLOCK) == odd)
        term = dot(picked, side)
        spread = term if spread is None else spread + term
    mask_out[...] = spread
    ready_out[...] = spread[0:8]


def edge_kernel(sea, air, sea_c, air_c, place, pair_out, next_out, first, last, sems):
    fields = 4
    copies = []
    for n, (state, courant) in enumerate(((sea, sea_c), (air, air_c))):
        size = courant.shape[0]
        for at in range(fields + 1):
            source, base = (state, at * size) if at < fields else (courant, 0)
            for side, (buf, start) in enumerate(((first, 0), (last, size - 8))):
                copies.append(
                    pltpu.make_async_copy(
                        source.at[pl.ds(base + start, 8)], buf.at[n, at], sems.at[n, at, side]
                    )
                )
    for copy in copies:
        copy.start()
    for copy in copies:
        copy.wait()
    for n in range(2):
        for at in range(fields + 1):
            row = n * 2 * (fields + 1) + 2 * at
            low, high = first[n, at, 0:2, :], last[n, at, 6:8, :]
            pair_out[row : row + 2, :] = jnp.where(place[0] // 4 == 0, high, low)
            next_out[row : row + 2, :] = jnp.where(place[0] // 4 == 0, low, high)


def neighbours(pair, other, place):
    pair, other = pair.get()[...], other.get()[...]
    even = place[0] // 4 == 0
    return jnp.where(even, other, pair), jnp.where(even, pair, other)


def stepped(x, low, high, positive, negative, buf):
    rows = x.shape[0]
    total = buf.shape[0]
    lane = iota((total, LANES), 1)
    first = lane == 0
    last = lane == LANES - 1
    buf[0:8, :] = jnp.broadcast_to(low, (8, LANES))
    buf[8 : rows + 8, :] = x
    buf[rows + 8 :, :] = jnp.broadcast_to(high, (8, LANES))
    x = buf[...]
    for step in range(2):
        below = pltpu.roll(x, 1, 1)
        below = jnp.where(first, pltpu.roll(below, 1, 0), below)
        above = pltpu.roll(x, LANES - 1, 1)
        above = jnp.where(last, pltpu.roll(above, total - 1, 0), above)
        x = x - positive * (x - below) - negative * (above - x)
    return x[8 : rows + 8, :]


def speeds(c, low, high, buf):
    rows = c.shape[0]
    buf[0:8, :] = jnp.broadcast_to(low, (8, LANES))
    buf[8 : rows + 8, :] = c
    buf[rows + 8 :, :] = jnp.broadcast_to(high, (8, LANES))
    c = buf[...]
    return jnp.maximum(c, 0.0), jnp.minimum(c, 0.0)


def upwind(x, positive, negative, below, above):
    return x - positive * (x - below) - negative * (above - x)


def sea_kernel(fields, state, courant, place, o0, o1, o2, o3, sbuf, sems):
    rows = courant.shape[0] // 2
    size = 2 * rows
    outs = (o0, o1, o2, o3)
    order = (1, 2, 3, 0)

    def copy(d):
        field = lax.rem(place[0] + d, fields)
        at = pl.multiple_of(field * size, size)
        return pltpu.make_async_copy(state.at[pl.ds(at, size)], sbuf.at[d], sems.at[d])

    for d in order:
        copy(d).start()
    lane = iota((rows, LANES), 1)
    first = lane == 0
    last = lane == LANES - 1
    courant = courant.get()
    c = courant[pl.ds(0, rows, stride=2), :]
    positive, negative = jnp.maximum(c, 0.0), jnp.minimum(c, 0.0)
    for d in order:
        copy(d).wait()
        out = outs[d]
        x = sbuf[d, pl.ds(0, rows, stride=2), :]
        for step in range(2):
            below = pltpu.roll(x, 1, 1)
            below = jnp.where(first, pltpu.roll(below, 1, 0), below)
            above = pltpu.roll(x, LANES - 1, 1)
            above = jnp.where(last, pltpu.roll(above, rows - 1, 0), above)
            x = upwind(x, positive, negative, below, above)
        out[0:rows, :] = x
        out[rows : rows + 1, :] = sbuf[d, 0:1, :]
        out[rows + 1 : rows + 2, :] = sbuf[d, size - 2 : size - 1, :]
        out[rows + 2 : rows + 3, :] = courant[0:1, :]
        out[rows + 3 : rows + 4, :] = courant[size - 2 : size - 1, :]
        out[rows + 4 : rows + 8, :] = jnp.zeros((4, LANES), F32)


def mended(first, last, left, right):
    low = low_half(first[0].shape)
    out = []
    for inner, outer, kept in ((first, left, low), (last, right, jnp.logical_not(low))):
        x = jnp.where(kept, inner[0], outer[0])
        c = jnp.where(kept, inner[1], outer[1])
        positive, negative = jnp.maximum(c, 0.0), jnp.minimum(c, 0.0)
        for step in range(2):
            x = upwind(x, positive, negative, pltpu.roll(x, 1, 1), pltpu.roll(x, LANES - 1, 1))
        out.append(x)
    return out


def mend(row, mended_row, at_end):
    lane = iota(row.shape, 1)
    return jnp.where(lane >= LANES - 2 if at_end else lane < 2, mended_row, row)


def outer_rows(halo, field, level, place):
    rows = (halo.shape[0] - 8) // 2
    pair, other = [
        (halo[pl.ds(n * rows + 2 * field + level, 1), :], halo[n * rows + 8 + level : n * rows + 9 + level, :])
        for n in range(2)
    ]
    even = place[0] // 4 == 0
    left = [jnp.where(even, b, a) for a, b in zip(pair, other)]
    right = [jnp.where(even, a, b) for a, b in zip(pair, other)]
    return left, right


def advect_kernel(
    fields, sea, air, sea_c, air_c, mixing, pair, other, lev,
    o0, o1, o2, o3, q0, q1, q2, q3, factor_out, lows, highs, xbuf, cbuf,
):
    rows = air_c.shape[0] // 2
    factor_out[...] = mixing.get()[pl.ds(0, rows, stride=8), :]
    lows[...], highs[...] = neighbours(pair, other, lev)
    levels = ((air, air_c, 1, 0), (air, air_c, 1, 1), (sea, sea_c, 0, 1))
    for n, (state, courant, part, level) in enumerate(levels):
        base = part * 2 * (fields + 1)
        c = courant.get()[pl.ds(level, rows, stride=2), :]
        at = base + 2 * fields + level
        positive, negative = speeds(c, lows[at : at + 1, :], highs[at : at + 1, :], cbuf)
        outs = (o0, o1, o2, o3) if part else (q0, q1, q2, q3)
        for d, out in enumerate(outs):
            field = lax.rem(lev[0] + d, fields)
            x = state.get()[pl.ds(field * 2 * rows + level, rows, stride=2), :]
            at = pl.ds(base + 2 * field + level, 1)
            x = stepped(x, lows[at, :], highs[at, :], positive, negative, xbuf)
            at = n * rows if part else 0
            out[at : at + rows, :] = x


def weight_copies(weight, wbuf, sems):
    pieces = sems.shape[0]
    size = weight.shape[0] // pieces
    return [
        pltpu.make_async_copy(
            weight.at[pl.ds(n * size, size)], wbuf.at[pl.ds(n * size, size)], sems.at[n]
        )
        for n in range(pieces)
    ]


def product_rows(values, ones, put):
    half = low_half(values.shape)
    zero = jnp.zeros(values.shape, F32)
    high = values.astype(BF16).astype(F32)
    sets = [(0, 2, high), (2, 2, values - high)]
    if ones is not None:
        sets.append((8, 0, ones))
    for base, gap, x in sets:
        turned = swap(x)
        for odd in range(2):
            for parity in range(2):
                row = base + odd * (2 + gap) + parity
                chosen = turned if odd != parity else x
                put(row, jnp.where(half == (parity == 0), chosen, zero))
    if ones is not None:
        for row in range(12, 16):
            put(row, zero)


def product_sums(got, with_ones):
    half = low_half(got(0).shape)
    out = [jnp.where(half, got(p) + got(2 + p), got(4 + p) + got(6 + p)) for p in range(2)]
    if with_ones:
        out.extend(jnp.where(half, got(8 + p), got(10 + p)) for p in range(2))
    return out


def products(values, ones, copies, wbuf, lhs, res):
    groups = values.shape[0]
    count = 8 if ones is None else 16

    def put(row, x):
        lhs[pl.ds(row, groups, stride=count), :] = x

    product_rows(values, ones, put)

    def body(step, carry):
        w = wbuf[pl.ds(pl.multiple_of(step * 2 * LANES, 2 * LANES), 2 * LANES), :]
        both = pl.ds(pl.multiple_of(step * 2 * count, 2 * count), 2 * count)
        out = dot(lhs[both, :].astype(BF16), w, NT)
        for n in range(2):
            at = pl.ds(pl.multiple_of((2 * step + n) * count, count), count)
            res[at, :] = out[n * count : (n + 1) * count, n * LANES : (n + 1) * LANES]
        return carry

    each = groups // 2 // len(copies)
    for n, copy in enumerate(copies):
        copy.wait()
        if n + AHEAD + 1 < len(copies):
            copies[n + AHEAD + 1].start()
        lax.fori_loop(n * each, (n + 1) * each, body, 0, unroll=each)
    return product_sums(lambda row: res[pl.ds(row, groups, stride=count), :], ones is not None)


def entry_order():
    row, column = iota((256, 512), 0), iota((256, 512), 1)
    same = ((row >> 6) & 1) * 2 + (row & 1) == (column >> 7)
    cell = ((row >> 1) & 31) * 2 + (row >> 7)
    return onehot(same & (cell == (column & 63)))


def entry_values(sums, order):
    def ordered(pair):
        high, low = split(jnp.concatenate(pair, 1))
        return dot(high, order), dot(low, order)

    y = ordered(sums[:2])
    if len(sums) > 2:
        half = low_half(y[0].shape[:1] + (LANES,))
        half = jnp.concatenate([half] * 4, 1)
        y = [jnp.where(half, a, b) for a, b in zip(y, ordered(sums[2:]))]
    terms = []
    for part in y:
        part = part.astype(BF16)
        terms.append(jnp.concatenate([part[:, q * LANES : (q + 1) * LANES] for q in range(4)], 0))
    return jnp.concatenate(terms, 1)


def slot_order(place):
    count = place.shape[1]
    return [onehot(iota((count, count), 0) == place[half : half + 1, :]) for half in range(2)]


def dispatched(orders, entries):
    out = []
    for order in orders:
        slots = dot(order, entries)
        out.append(slots[:, :LANES] + slots[:, LANES:])
    return out


def surface_copy(parts, at, lev, buf, sem):
    copies = [
        pltpu.make_async_copy(part.at[pl.ds(at, buf.shape[0])], buf, sem) for part in parts
    ]
    for d, copy in enumerate(copies):

        @pl.when(lev[0] % 4 == d)
        def start(copy=copy):
            copy.start()

    return copies[0]


def up_kernel(
    p0, p1, p2, p3, h0, h1, h2, h3, mask, place, labels, weight, lev,
    out, values, halo, wbuf, lhs, res, sems, wsems,
):
    tiles = labels.shape[0]
    rows = mask.shape[0]
    own = surface_copy((h0, h1, h2, h3), 0, lev, halo, sems.at[1])
    field = surface_copy((p0, p1, p2, p3), 0, lev, values, sems.at[0])
    copies = weight_copies(weight, wbuf, wsems)
    for copy in copies[:AHEAD]:
        copy.start()
    order = entry_order()
    slots = slot_order(place.get())
    field.wait()
    own.wait()
    copies[AHEAD].start()
    ends = values[rows:, :]
    mended_rows = mended(
        (ends[0:1], ends[2:3]), (ends[1:2], ends[3:4]), *outer_rows(halo, lev[0] % 4, 0, lev)
    )
    for n, at in enumerate((0, rows - 1)):
        values[at : at + 1, :] = mend(values[at : at + 1, :], mended_rows[n], n == 1)
    mask_value = mask.get()[...]
    sums = products(values[0:rows, :] * mask_value, mask_value, copies, wbuf, lhs, res)
    even, odd = dispatched(slots, entry_values(sums, order))
    half = low_half((tiles, LANES))
    pitch = out.shape[0] // tiles
    for i in range(SLOTS // 2):
        a, b = even[i * tiles : (i + 1) * tiles], odd[i * tiles : (i + 1) * tiles]
        out[pl.ds(i, tiles, stride=pitch), :] = jnp.where(half, a, swap(b))
        out[pl.ds(SLOTS // 2 + i, tiles, stride=pitch), :] = jnp.where(half, swap(a), b)
    out[pl.ds(SLOTS, tiles, stride=pitch), :] = labels.get()[...]


def named_blocks(labels, base, blocks):
    turned = jnp.transpose(jnp.concatenate([labels, labels], 0))
    half = low_half((1, LANES))
    out = []
    for slot_half in range(2):
        row = []
        for i in range(0, SLOTS // 2, 2):
            at = base + 2 * i + slot_half
            row.append(jnp.where(half, turned[at : at + 1], turned[at + 2 : at + 3]))
        row = jnp.concatenate(row, 1).astype(jnp.int32)
        for odd in range(2):
            out.append(onehot(2 * iota((blocks, row.shape[1]), 0) + odd + 1 == row))
    return out


def collected(parts, names):
    halves = []
    for part in parts:
        halves.extend(split(part))
    values = jnp.concatenate(halves, 1)
    sums = [dot(name, values) for name in names]
    half = low_half((sums[0].shape[0], LANES))
    out = []
    for n in range(len(parts)):
        at = 2 * n * LANES
        g = [s[:, at : at + LANES] + s[:, at + LANES : at + 2 * LANES] for s in sums]
        out.append(jnp.where(half, g[0] + swap(g[2]), swap(g[1]) + g[3]))
    return out


def slot_rows(arrived, start, count, tiles):
    pitch = arrived.shape[0] // tiles
    return jnp.concatenate(
        [arrived[pl.ds(start + i, tiles, stride=pitch), :] for i in range(count)], 0
    )


def middle_kernel(
    arrived, p0, p1, p2, p3, factor, place, weight, lev,
    flux_out, out, label_out, values, wbuf, lhs, res, sem, wsems,
):
    groups = flux_out.shape[0]
    tiles = label_out.shape[0]
    surface = surface_copy((p0, p1, p2, p3), 0, lev, values, sem)
    copies = weight_copies(weight, wbuf, wsems)
    for copy in copies[:AHEAD]:
        copy.start()
    order = entry_order()
    slots = slot_order(place.get())
    arrived = arrived.get()
    copies[AHEAD].start()
    labels = arrived[pl.ds(SLOTS, tiles, stride=SLOTS + 1), :]
    label_out[...] = labels
    names = named_blocks(labels, 0, groups)
    field = slot_rows(arrived, 0, SLOTS // 2, tiles)
    cover = slot_rows(arrived, SLOTS // 2, SLOTS // 2, tiles)
    received, coverage = collected((field, cover), names)
    surface.wait()
    flux = factor.get()[...] * (coverage * values[...] - received)
    flux_out[...] = flux
    sums = products(flux, None, copies, wbuf, lhs, res)
    even, odd = dispatched(slots, entry_values(sums, order))
    half = low_half((tiles, LANES))
    pitch = out.shape[0] // tiles
    for i in range(SLOTS // 2):
        a, b = even[i * tiles : (i + 1) * tiles], odd[i * tiles : (i + 1) * tiles]
        out[pl.ds(i, tiles, stride=pitch), :] = jnp.where(half, a, b)


def solve_kernel(with_flux, p0, p1, p2, p3, *refs):
    rest = (p0, p1, p2, p3)
    if with_flux:
        mixing, extra, lev, out, buf, sems = refs
        groups = extra.shape[0]
        moves = [(rest, 0, 2 * groups, buf, 0)]
    else:
        *more, mixing, extra, lev, out, unit_out, buf, halo, sems = refs
        groups = extra.shape[0]
        moves = [
            (rest, 0, groups, buf, groups),
            (more[:4], 0, groups, buf, 0),
            (more[:4], groups, 8, buf, 2 * groups),
            (more[4:], 0, halo.shape[1], halo, 0),
        ]
    chunk = 16
    levels = 8
    copies = []
    for n, (parts, at, count, to, base) in enumerate(moves):
        for d, part in enumerate(parts):
            source = lax.rem(lev[0] + 4 - d, 4)
            copies.append(
                pltpu.make_async_copy(
                    part.at[pl.ds(at, count)], to.at[source, pl.ds(base, count)], sems.at[n, d]
                )
            )
    for copy in copies:
        copy.start()
    kbuf, ebuf = mixing.get(), extra.get()
    for copy in copies:
        copy.wait()
    if not with_flux:
        parts = [[[], []] for n in range(4)]
        for source in range(levels // 2):
            ends = [buf[source, 2 * groups + n : 2 * groups + n + 1, :] for n in range(4)]
            left, right = outer_rows(halo.at[source], lev[0] % 4, 0, lev)
            for n, rows in enumerate(((ends[0], ends[2]), (ends[1], ends[3]), left, right)):
                parts[n][0].append(rows[0])
                parts[n][1].append(rows[1])
        mended_rows = mended(*[[jnp.concatenate(rows, 0) for rows in part] for part in parts])
        for source in range(levels // 2):
            for n, row in enumerate((0, groups - 1)):
                old = buf[source, row : row + 1, :]
                new = mended_rows[n][source : source + 1]
                buf[source, row : row + 1, :] = mend(old, new, n == 1)

    def body(step, carry):
        at = pl.multiple_of(step * chunk, chunk)
        rows = pl.ds(at, chunk)
        k = [
            kbuf[pl.ds(at * levels + level, chunk, stride=levels), :] for level in range(levels)
        ]
        cs, ds, es = [], [], []
        for level in range(levels):
            r = buf[level // 2, pl.ds((level % 2) * groups + at, chunk), :]
            if level == 0:
                inverse = 1.0 / (1.0 + k[1])
                if with_flux:
                    r = r - ebuf[rows, :]
                else:
                    es.append(k[0] * ebuf[rows, :] * inverse)
                ds.append(r * inverse)
            else:
                total = 1.0 + k[level] - k[level] * cs[-1]
                if level + 1 < levels:
                    total = total + k[level + 1]
                inverse = 1.0 / total
                ds.append((r + k[level] * ds[-1]) * inverse)
                if not with_flux:
                    es.append(k[level] * es[-1] * inverse)
            if level + 1 < levels:
                cs.append(k[level + 1] * inverse)
        for terms, ref in ((ds, out),) if with_flux else ((ds, out), (es, unit_out)):
            x = terms[-1]
            ref[pl.ds(at * levels + levels - 1, chunk, stride=levels), :] = x
            for level in range(levels - 2, -1, -1):
                x = terms[level] + cs[level] * x
                ref[pl.ds(at * levels + level, chunk, stride=levels), :] = x
        return carry

    lax.fori_loop(0, groups // chunk, body, 0)


def last_kernel(arrived, labels, base, unit, out, gain, obuf, sems):
    tiles = labels.shape[0]
    groups = gain.shape[0]
    names = named_blocks(labels.get()[...], SLOTS, groups)
    (total,) = collected((slot_rows(arrived.get(), 0, SLOTS // 2, tiles),), names)
    gain[...] = total
    bbuf, ubuf = base.get(), unit.get()

    def body(step, carry):
        at = pl.ds(pl.multiple_of(step * 8, 8), 8)
        obuf[at, :] = bbuf[at, :] + ubuf[at, :] * gain[pl.ds(step, 1), :]
        return carry

    pieces = sems.shape[0]
    copies = []
    for n in range(pieces):
        lax.fori_loop(n * groups // pieces, (n + 1) * groups // pieces, body, 0, unroll=8)
        rows = pl.ds(n * 8 * groups // pieces, 8 * groups // pieces)
        copies.append(pltpu.make_async_copy(obuf.at[rows], out.at[rows], sems.at[n]))
        copies[n].start()
    for copy in copies:
        copy.wait()


VMEM = pl.BlockSpec(memory_space=pltpu.VMEM)
SMEM = pl.BlockSpec(memory_space=pltpu.SMEM)
HBM = pl.BlockSpec(memory_space=pltpu.HBM)
DMA = pltpu.SemaphoreType.DMA


def call(kernel, shapes, args, spaces, scratch=(), name=None, us=1.0, after=(), to=None):
    fetched = [i for i, space in enumerate(spaces) if space == "f"]
    outs = len(shapes) if isinstance(shapes, tuple) else 1

    def body(*refs):
        refs = list(refs)
        del refs[len(args) : len(args) + len(after)]
        end = len(refs) - 2 * len(fetched)
        for n, i in enumerate(fetched):
            refs[i] = Fetched(refs[i], refs[end + n], refs[end + len(fetched) + n])
        kernel(*refs[:end])

    extra = [pltpu.VMEM(args[i].shape, args[i].dtype) for i in fetched]
    extra += [DMA(()) for i in fetched]
    return pl.pallas_call(
        body,
        out_shape=shapes,
        in_specs=[{"v": VMEM, "s": SMEM, "h": HBM, "f": HBM}[space] for space in spaces]
        + [HBM] * len(after),
        out_specs=jax.tree.map(lambda _: VMEM, shapes) if to is None else to,
        scratch_shapes=list(scratch) + extra,
        compiler_params=pltpu.CompilerParams(vmem_limit_bytes=64 * 1024 * 1024),
        cost_estimate=pl.CostEstimate(
            flops=0, bytes_accessed=int(us * 3.6e6), transcendentals=0
        ),
        name=name,
    )(*args, *after)


def shape(*dims, dtype=F32):
    return jax.ShapeDtypeStruct(dims, dtype)


def tile_rows(x, lead):
    levels, cells = x.shape[-2:]
    x = x.reshape(lead, levels, cells // LANES, LANES)
    return x.transpose(0, 2, 1, 3).reshape(lead * levels * cells // LANES, LANES)


def weight_rows(w):
    blocks, fan, size = w.shape
    w = w.reshape(blocks, fan, size // LANES, LANES).transpose(0, 2, 1, 3)
    return w.reshape(blocks * fan * size // LANES, LANES)


def on_device(
    air_state,
    sea_state,
    air_courant,
    sea_courant,
    air_mixing,
    sea_mixing,
    upward_weight,
    upward_target,
    upward_block,
    downward_weight,
    downward_target,
    downward_block,
    sea_mask,
):
    fields, pair, cells = air_state.shape
    tiles = lax.axis_size("tiles")
    levs = lax.axis_size("lev")
    rows = cells // LANES
    groups = sea_mask.shape[0] // 2
    lev = lax.axis_index("lev").astype(jnp.int32)
    tile = lax.axis_index("tiles").astype(jnp.int32)
    lev_ref = (lev + levs * (tile % 2)).reshape(1)
    states = (
        tile_rows(sea_state, fields),
        tile_rows(air_state, fields),
        tile_rows(sea_courant, 1),
        tile_rows(air_courant, 1),
    )
    size = pair * rows

    to_pair, to_other = call(
        edge_kernel,
        (shape(20, LANES),) * 2,
        (*states, lev_ref),
        "hhhhs",
        scratch=[
            pltpu.VMEM((2, fields + 1, 8, LANES), F32),
            pltpu.VMEM((2, fields + 1, 8, LANES), F32),
            DMA((2, fields + 1, 2)),
        ],
        name="edges",
        us=1.5,
    )
    pairs = [(i, i + 1 - 2 * (i % 2)) for i in range(tiles)]
    others = [(i, (i - 1 + 2 * (i % 2)) % tiles) for i in range(tiles)]
    ends = (
        lax.ppermute(to_pair, "tiles", pairs),
        lax.ppermute(to_other, "tiles", others),
    )
    extended = pltpu.VMEM((rows + 16, LANES), F32)

    def around(parts):
        return [parts[0]] + [
            lax.ppermute(parts[d], "lev", [(i, (i + d) % levs) for i in range(levs)])
            for d in range(1, levs)
        ]

    sea_own = call(
        functools.partial(sea_kernel, fields),
        (shape(rows + 8, LANES),) * 4,
        (states[0], states[2], lev_ref),
        "hfs",
        scratch=[pltpu.VMEM((4, size, LANES), F32), DMA((4,))],
        name="sea",
        us=3.0,
        after=(to_pair,),
    )
    sea = around(sea_own)
    entries = 4 * groups
    place_up, place_down, labels, mask, ready = call(
        functools.partial(prepare_kernel, tiles),
        (
            shape(2, entries, dtype=jnp.int32),
            shape(2, entries, dtype=jnp.int32),
            shape(tiles, LANES),
            shape(groups, LANES),
            shape(8, LANES),
        ),
        (
            upward_target.T,
            upward_block.T,
            downward_target.T,
            downward_block.T,
            sea_mask.reshape(1, -1),
        ),
        "fffff",
        name="prepare",
        us=2.5,
        after=(sea_own[0],),
    )
    halo = around([jnp.concatenate([*ends, ready], 0)] * 4)
    air_k = tile_rows(air_mixing, 1)
    sea_k = tile_rows(sea_mixing, 1)
    up_rows = weight_rows(upward_weight)
    down_rows = weight_rows(downward_weight)

    def workspace(count):
        return [
            pltpu.VMEM(up_rows.shape, BF16),
            pltpu.VMEM((groups * count, LANES), F32),
            pltpu.VMEM((groups * count, LANES), F32),
        ]

    pitch = SLOTS + 1
    outgoing = call(
        up_kernel,
        shape(tiles * pitch, LANES),
        (*sea, *halo, mask, place_up, labels, up_rows, lev_ref),
        "hhhhhhhhfffhs",
        scratch=[
            pltpu.VMEM((rows + 8, LANES), F32),
            pltpu.VMEM(halo[0].shape, F32),
            *workspace(16),
            DMA((2,)),
            DMA((PIECES,)),
        ],
        name="upward",
        us=8.0,
    )

    def over_tiles(x):
        pitch = x.shape[0] // tiles
        y = x.reshape((tiles, pitch, LANES) if pitch % 8 == 0 else (tiles, 1, pitch * LANES))
        y = lax.all_to_all(y, "tiles", split_axis=0, concat_axis=0, tiled=True)
        return y.reshape(x.shape)

    *rest, factor = call(
        functools.partial(advect_kernel, fields),
        (shape(size, LANES),) * 4 + (shape(rows, LANES),) * 5,
        (*states, air_k, *ends, lev_ref),
        "fffffffs",
        scratch=[pltpu.VMEM((20, LANES), F32)] * 2 + [extended, extended],
        name="advect",
        us=4.0,
        after=(outgoing,),
    )
    air = around(rest[:4])
    arrived = over_tiles(outgoing)
    flux, returning, labels_down = call(
        middle_kernel,
        (shape(groups, LANES), shape(tiles * SLOTS // 2, LANES), shape(tiles, LANES)),
        (arrived, *air, factor, place_down, down_rows, lev_ref),
        "fhhhhffhs",
        scratch=[pltpu.VMEM((rows, LANES), F32), *workspace(8), DMA(()), DMA((PIECES,))],
        name="middle",
        us=8.0,
    )
    gained = over_tiles(returning)
    sea_rest = around(rest[4:])

    column = shape(8 * rows, LANES)

    def solve(with_flux, parts, k, extra, name, after=()):
        buf = pltpu.VMEM((4, 2 * rows if with_flux else 2 * rows + 8, LANES), F32)
        return call(
            functools.partial(solve_kernel, with_flux),
            column if with_flux else (column, column),
            (*parts, k, extra, lev_ref),
            "h" * len(parts) + "ffs",
            scratch=[
                buf,
                *([] if with_flux else [pltpu.VMEM((4, *halo[0].shape), F32)]),
                DMA((1 if with_flux else 4, 4)),
            ],
            name=name,
            us=3.0,
            after=after,
        )

    air_out = solve(True, air, air_k, flux, "solve_air")
    base, unit = solve(False, [*sea_rest, *sea, *halo], sea_k, mask, "solve_sea", (air_out,))
    sea_out = call(
        last_kernel,
        column,
        (gained, labels_down, base, unit),
        "ffff",
        scratch=[pltpu.VMEM((rows, LANES), F32), pltpu.VMEM((8 * rows, LANES), F32), DMA((4,))],
        name="last",
        to=HBM,
        us=2.0,
    )

    def levels_first(x):
        return x.reshape(rows, 8, LANES).transpose(1, 0, 2).reshape(1, 8, cells)

    return levels_first(air_out), levels_first(sea_out)


def solution(mesh):
    return jax.shard_map(
        on_device,
        mesh=mesh,
        in_specs=(
            P(None, "lev", "tiles"),
            P(None, "lev", "tiles"),
            P("lev", "tiles"),
            P("lev", "tiles"),
            P(None, "tiles"),
            P(None, "tiles"),
            P("tiles", None, None),
            P("tiles", None),
            P("tiles", None),
            P("tiles", None, None),
            P("tiles", None),
            P("tiles", None),
            P("tiles"),
        ),
        out_specs=(P("lev", None, "tiles"), P("lev", None, "tiles")),
        check_vma=False,
    )
```

```python
import functools

import jax
import jax.numpy as jnp
from jax import lax
from jax.experimental import pallas as pl
from jax.experimental.pallas import tpu as pltpu
from jax.sharding import PartitionSpec as P

BLOCK = 64
LANES = 128
SLOTS = 16
PIECES = 4
AHEAD = 2
F32 = jnp.float32
BF16 = jnp.bfloat16
NT = (((1,), (1,)), ((), ()))
NN = (((1,), (0,)), ((), ()))


def dot(a, b, dims=NN):
    return lax.dot_general(a, b, dims, preferred_element_type=F32)


def split(x):
    high = x.astype(BF16)
    return high, (x - high.astype(F32)).astype(BF16)


def iota(shape, dim):
    return lax.broadcasted_iota(jnp.int32, shape, dim)


def low_half(shape):
    return iota(shape, len(shape) - 1) < BLOCK


def swap(x):
    return pltpu.roll(x, BLOCK, x.ndim - 1)


class Fetched:
    def __init__(self, source, buf, sem):
        self.copy = pltpu.make_async_copy(source, buf, sem)
        self.shape = source.shape
        self.buf = buf
        self.waiting = True
        self.copy.start()

    def get(self):
        if self.waiting:
            self.copy.wait()
            self.waiting = False
        return self.buf


def onehot(condition):
    return jnp.where(condition, 1.0, 0.0).astype(BF16)


def prepare_kernel(
    tiles, ut, ub, dt, db, mask, up_out, down_out, label_out, mask_out, ready_out
):
    blocks = ut.shape[1]
    groups = blocks // 2
    entries = 2 * blocks
    source, lane = iota((blocks, blocks), 0), iota((blocks, blocks), 1)
    turn = onehot(source == 2 * (lane & (groups - 1)) + lane // groups)
    lists = [x.get()[...] for x in (ut, ub, dt, db, mask)]
    stacked = jnp.concatenate([x.astype(F32) for x in lists], 0)
    stacked = jnp.concatenate([stacked, jnp.zeros((16 - stacked.shape[0], blocks), F32)], 0)
    stacked = dot(stacked.astype(BF16), turn)

    def entry_row(at):
        pair = stacked[at : at + 2]
        parts = [
            pair[k : k + 1, odd * groups : (odd + 1) * groups]
            for odd in range(2)
            for k in range(2)
        ]
        return jnp.concatenate(parts, 1)

    tile_row = iota((tiles, entries), 0).astype(F32)
    earlier = onehot(iota((entries, entries), 0) < iota((entries, entries), 1))
    labels = None
    for first, out, base in ((0, up_out, 0), (4, down_out, SLOTS)):
        target, block = entry_row(first), entry_row(first + 2)
        named = jnp.where(target == tile_row, 1.0, 0.0)
        rank = jnp.sum(named * dot(named.astype(BF16), earlier), 0, keepdims=True)
        rank = rank.astype(jnp.int32)
        target = target.astype(jnp.int32)
        at = (rank // 2) * tiles + target
        for half in range(2):
            out[half : half + 1, :] = jnp.where((rank & 1) == half, at, -1)
        carried = (named * (block + 1.0)).astype(BF16)
        chosen = onehot(iota((LANES, entries), 0) == rank + base)
        term = dot(carried, chosen, NT)
        labels = term if labels is None else labels + term
    label_out[...] = labels
    diagonal = iota((groups, groups), 0) == iota((groups, groups), 1)
    spread = None
    for odd in range(2):
        row = stacked[8:9, odd * groups : (odd + 1) * groups]
        picked = jnp.where(diagonal, row, 0.0).astype(BF16)
        side = onehot((iota((groups, LANES), 1) // BLOCK) == odd)
        term = dot(picked, side)
        spread = term if spread is None else spread + term
    mask_out[...] = spread
    ready_out[...] = spread[0:8]


def edge_kernel(sea, air, sea_c, air_c, place, pair_out, next_out, first, last, sems):
    fields = 4
    copies = []
    for n, (state, courant) in enumerate(((sea, sea_c), (air, air_c))):
        size = courant.shape[0]
        for at in range(fields + 1):
            source, base = (state, at * size) if at < fields else (courant, 0)
            for side, (buf, start) in enumerate(((first, 0), (last, size - 8))):
                copies.append(
                    pltpu.make_async_copy(
                        source.at[pl.ds(base + start, 8)], buf.at[n, at], sems.at[n, at, side]
                    )
                )
    for copy in copies:
        copy.start()
    for copy in copies:
        copy.wait()
    for n in range(2):
        for at in range(fields + 1):
            row = n * 2 * (fields + 1) + 2 * at
            low, high = first[n, at, 0:2, :], last[n, at, 6:8, :]
            pair_out[row : row + 2, :] = jnp.where(place[0] // 4 == 0, high, low)
            next_out[row : row + 2, :] = jnp.where(place[0] // 4 == 0, low, high)


def neighbours(pair, other, place):
    pair, other = pair.get()[...], other.get()[...]
    even = place[0] // 4 == 0
    return jnp.where(even, other, pair), jnp.where(even, pair, other)


def stepped(x, low, high, positive, negative, buf):
    rows = x.shape[0]
    total = buf.shape[0]
    lane = iota((total, LANES), 1)
    first = lane == 0
    last = lane == LANES - 1
    buf[0:8, :] = jnp.broadcast_to(low, (8, LANES))
    buf[8 : rows + 8, :] = x
    buf[rows + 8 :, :] = jnp.broadcast_to(high, (8, LANES))
    x = buf[...]
    for step in range(2):
        below = pltpu.roll(x, 1, 1)
        below = jnp.where(first, pltpu.roll(below, 1, 0), below)
        above = pltpu.roll(x, LANES - 1, 1)
        above = jnp.where(last, pltpu.roll(above, total - 1, 0), above)
        x = x - positive * (x - below) - negative * (above - x)
    return x[8 : rows + 8, :]


def speeds(c, low, high, buf):
    rows = c.shape[0]
    buf[0:8, :] = jnp.broadcast_to(low, (8, LANES))
    buf[8 : rows + 8, :] = c
    buf[rows + 8 :, :] = jnp.broadcast_to(high, (8, LANES))
    c = buf[...]
    return jnp.maximum(c, 0.0), jnp.minimum(c, 0.0)


def upwind(x, positive, negative, below, above):
    return x - positive * (x - below) - negative * (above - x)


def sea_kernel(fields, state, courant, place, o0, o1, o2, o3, sbuf, sems):
    rows = courant.shape[0] // 2
    size = 2 * rows
    outs = (o0, o1, o2, o3)
    order = (1, 2, 3, 0)

    def copy(d):
        field = lax.rem(place[0] + d, fields)
        at = pl.multiple_of(field * size, size)
        return pltpu.make_async_copy(state.at[pl.ds(at, size)], sbuf.at[d], sems.at[d])

    for d in order:
        copy(d).start()
    lane = iota((rows, LANES), 1)
    first = lane == 0
    last = lane == LANES - 1
    courant = courant.get()
    c = courant[pl.ds(0, rows, stride=2), :]
    positive, negative = jnp.maximum(c, 0.0), jnp.minimum(c, 0.0)
    for d in order:
        copy(d).wait()
        out = outs[d]
        x = sbuf[d, pl.ds(0, rows, stride=2), :]
        for step in range(2):
            below = pltpu.roll(x, 1, 1)
            below = jnp.where(first, pltpu.roll(below, 1, 0), below)
            above = pltpu.roll(x, LANES - 1, 1)
            above = jnp.where(last, pltpu.roll(above, rows - 1, 0), above)
            x = upwind(x, positive, negative, below, above)
        out[0:rows, :] = x
        out[rows : rows + 1, :] = sbuf[d, 0:1, :]
        out[rows + 1 : rows + 2, :] = sbuf[d, size - 2 : size - 1, :]
        out[rows + 2 : rows + 3, :] = courant[0:1, :]
        out[rows + 3 : rows + 4, :] = courant[size - 2 : size - 1, :]
        out[rows + 4 : rows + 8, :] = jnp.zeros((4, LANES), F32)


def mended(first, last, left, right):
    low = low_half(first[0].shape)
    out = []
    for inner, outer, kept in ((first, left, low), (last, right, jnp.logical_not(low))):
        x = jnp.where(kept, inner[0], outer[0])
        c = jnp.where(kept, inner[1], outer[1])
        positive, negative = jnp.maximum(c, 0.0), jnp.minimum(c, 0.0)
        for step in range(2):
            x = upwind(x, positive, negative, pltpu.roll(x, 1, 1), pltpu.roll(x, LANES - 1, 1))
        out.append(x)
    return out


def mend(row, mended_row, at_end):
    lane = iota(row.shape, 1)
    return jnp.where(lane >= LANES - 2 if at_end else lane < 2, mended_row, row)


def outer_rows(halo, field, level, place):
    rows = (halo.shape[0] - 8) // 2
    pair, other = [
        (halo[pl.ds(n * rows + 2 * field + level, 1), :], halo[n * rows + 8 + level : n * rows + 9 + level, :])
        for n in range(2)
    ]
    even = place[0] // 4 == 0
    left = [jnp.where(even, b, a) for a, b in zip(pair, other)]
    right = [jnp.where(even, a, b) for a, b in zip(pair, other)]
    return left, right


def advect_kernel(
    fields, sea, air, sea_c, air_c, mixing, pair, other, lev,
    o0, o1, o2, o3, q0, q1, q2, q3, factor_out, lows, highs, xbuf, cbuf,
):
    rows = air_c.shape[0] // 2
    factor_out[...] = mixing.get()[pl.ds(0, rows, stride=8), :]
    lows[...], highs[...] = neighbours(pair, other, lev)
    levels = ((air, air_c, 1, 0), (air, air_c, 1, 1), (sea, sea_c, 0, 1))
    for n, (state, courant, part, level) in enumerate(levels):
        base = part * 2 * (fields + 1)
        c = courant.get()[pl.ds(level, rows, stride=2), :]
        at = base + 2 * fields + level
        positive, negative = speeds(c, lows[at : at + 1, :], highs[at : at + 1, :], cbuf)
        outs = (o0, o1, o2, o3) if part else (q0, q1, q2, q3)
        for d, out in enumerate(outs):
            field = lax.rem(lev[0] + d, fields)
            x = state.get()[pl.ds(field * 2 * rows + level, rows, stride=2), :]
            at = pl.ds(base + 2 * field + level, 1)
            x = stepped(x, lows[at, :], highs[at, :], positive, negative, xbuf)
            at = n * rows if part else 0
            out[at : at + rows, :] = x


def weight_copies(weight, wbuf, sems):
    pieces = sems.shape[0]
    size = weight.shape[0] // pieces
    return [
        pltpu.make_async_copy(
            weight.at[pl.ds(n * size, size)], wbuf.at[pl.ds(n * size, size)], sems.at[n]
        )
        for n in range(pieces)
    ]


def product_rows(values, ones, put):
    half = low_half(values.shape)
    zero = jnp.zeros(values.shape, F32)
    high = values.astype(BF16).astype(F32)
    sets = [(0, 2, high), (2, 2, values - high)]
    if ones is not None:
        sets.append((8, 0, ones))
    for base, gap, x in sets:
        turned = swap(x)
        for odd in range(2):
            for parity in range(2):
                row = base + odd * (2 + gap) + parity
                chosen = turned if odd != parity else x
                put(row, jnp.where(half == (parity == 0), chosen, zero))
    if ones is not None:
        for row in range(12, 16):
            put(row, zero)


def product_sums(got, with_ones):
    half = low_half(got(0).shape)
    out = [jnp.where(half, got(p) + got(2 + p), got(4 + p) + got(6 + p)) for p in range(2)]
    if with_ones:
        out.extend(jnp.where(half, got(8 + p), got(10 + p)) for p in range(2))
    return out


def products(values, ones, copies, wbuf, lhs, res):
    groups = values.shape[0]
    count = 8 if ones is None else 16

    def put(row, x):
        lhs[pl.ds(row, groups, stride=count), :] = x

    product_rows(values, ones, put)

    def body(step, carry):
        w = wbuf[pl.ds(pl.multiple_of(step * 2 * LANES, 2 * LANES), 2 * LANES), :]
        both = pl.ds(pl.multiple_of(step * 2 * count, 2 * count), 2 * count)
        out = dot(lhs[both, :].astype(BF16), w, NT)
        for n in range(2):
            at = pl.ds(pl.multiple_of((2 * step + n) * count, count), count)
            res[at, :] = out[n * count : (n + 1) * count, n * LANES : (n + 1) * LANES]
        return carry

    each = groups // 2 // len(copies)
    for n, copy in enumerate(copies):
        copy.wait()
        if n + AHEAD + 1 < len(copies):
            copies[n + AHEAD + 1].start()
        lax.fori_loop(n * each, (n + 1) * each, body, 0, unroll=each)
    return product_sums(lambda row: res[pl.ds(row, groups, stride=count), :], ones is not None)


def entry_order():
    row, column = iota((256, 512), 0), iota((256, 512), 1)
    same = ((row >> 6) & 1) * 2 + (row & 1) == (column >> 7)
    cell = ((row >> 1) & 31) * 2 + (row >> 7)
    return onehot(same & (cell == (column & 63)))


def entry_values(sums, order):
    def ordered(pair):
        high, low = split(jnp.concatenate(pair, 1))
        return dot(high, order), dot(low, order)

    y = ordered(sums[:2])
    if len(sums) > 2:
        half = low_half(y[0].shape[:1] + (LANES,))
        half = jnp.concatenate([half] * 4, 1)
        y = [jnp.where(half, a, b) for a, b in zip(y, ordered(sums[2:]))]
    terms = []
    for part in y:
        part = part.astype(BF16)
        terms.append(jnp.concatenate([part[:, q * LANES : (q + 1) * LANES] for q in range(4)], 0))
    return jnp.concatenate(terms, 1)


def slot_order(place):
    count = place.shape[1]
    return [onehot(iota((count, count), 0) == place[half : half + 1, :]) for half in range(2)]


def dispatched(orders, entries):
    out = []
    for order in orders:
        slots = dot(order, entries)
        out.append(slots[:, :LANES] + slots[:, LANES:])
    return out


def surface_copy(parts, at, lev, buf, sem):
    copies = [
        pltpu.make_async_copy(part.at[pl.ds(at, buf.shape[0])], buf, sem) for part in parts
    ]
    for d, copy in enumerate(copies):

        @pl.when(lev[0] % 4 == d)
        def start(copy=copy):
            copy.start()

    return copies[0]


def up_kernel(
    p0, p1, p2, p3, h0, h1, h2, h3, mask, place, labels, weight, lev,
    out, values, halo, wbuf, lhs, res, sems, wsems,
):
    tiles = labels.shape[0]
    rows = mask.shape[0]
    own = surface_copy((h0, h1, h2, h3), 0, lev, halo, sems.at[1])
    field = surface_copy((p0, p1, p2, p3), 0, lev, values, sems.at[0])
    copies = weight_copies(weight, wbuf, wsems)
    for copy in copies[:AHEAD]:
        copy.start()
    order = entry_order()
    slots = slot_order(place.get())
    field.wait()
    own.wait()
    copies[AHEAD].start()
    ends = values[rows:, :]
    mended_rows = mended(
        (ends[0:1], ends[2:3]), (ends[1:2], ends[3:4]), *outer_rows(halo, lev[0] % 4, 0, lev)
    )
    for n, at in enumerate((0, rows - 1)):
        values[at : at + 1, :] = mend(values[at : at + 1, :], mended_rows[n], n == 1)
    mask_value = mask.get()[...]
    sums = products(values[0:rows, :] * mask_value, mask_value, copies, wbuf, lhs, res)
    even, odd = dispatched(slots, entry_values(sums, order))
    half = low_half((tiles, LANES))
    pitch = out.shape[0] // tiles
    for i in range(SLOTS // 2):
        a, b = even[i * tiles : (i + 1) * tiles], odd[i * tiles : (i + 1) * tiles]
        out[pl.ds(i, tiles, stride=pitch), :] = jnp.where(half, a, swap(b))
        out[pl.ds(SLOTS // 2 + i, tiles, stride=pitch), :] = jnp.where(half, swap(a), b)
    out[pl.ds(SLOTS, tiles, stride=pitch), :] = labels.get()[...]


def named_blocks(labels, base, blocks):
    turned = jnp.transpose(jnp.concatenate([labels, labels], 0))
    half = low_half((1, LANES))
    out = []
    for slot_half in range(2):
        row = []
        for i in range(0, SLOTS // 2, 2):
            at = base + 2 * i + slot_half
            row.append(jnp.where(half, turned[at : at + 1], turned[at + 2 : at + 3]))
        row = jnp.concatenate(row, 1).astype(jnp.int32)
        for odd in range(2):
            out.append(onehot(2 * iota((blocks, row.shape[1]), 0) + odd + 1 == row))
    return out


def collected(parts, names):
    halves = []
    for part in parts:
        halves.extend(split(part))
    values = jnp.concatenate(halves, 1)
    sums = [dot(name, values) for name in names]
    half = low_half((sums[0].shape[0], LANES))
    out = []
    for n in range(len(parts)):
        at = 2 * n * LANES
        g = [s[:, at : at + LANES] + s[:, at + LANES : at + 2 * LANES] for s in sums]
        out.append(jnp.where(half, g[0] + swap(g[2]), swap(g[1]) + g[3]))
    return out


def slot_rows(arrived, start, count, tiles):
    pitch = arrived.shape[0] // tiles
    return jnp.concatenate(
        [arrived[pl.ds(start + i, tiles, stride=pitch), :] for i in range(count)], 0
    )


def middle_kernel(
    arrived, p0, p1, p2, p3, factor, place, weight, lev,
    flux_out, out, label_out, values, wbuf, lhs, res, sem, wsems,
):
    groups = flux_out.shape[0]
    tiles = label_out.shape[0]
    surface = surface_copy((p0, p1, p2, p3), 0, lev, values, sem)
    copies = weight_copies(weight, wbuf, wsems)
    for copy in copies[:AHEAD]:
        copy.start()
    order = entry_order()
    slots = slot_order(place.get())
    arrived = arrived.get()
    copies[AHEAD].start()
    labels = arrived[pl.ds(SLOTS, tiles, stride=SLOTS + 1), :]
    label_out[...] = labels
    names = named_blocks(labels, 0, groups)
    field = slot_rows(arrived, 0, SLOTS // 2, tiles)
    cover = slot_rows(arrived, SLOTS // 2, SLOTS // 2, tiles)
    received, coverage = collected((field, cover), names)
    surface.wait()
    flux = factor.get()[...] * (coverage * values[...] - received)
    flux_out[...] = flux
    sums = products(flux, None, copies, wbuf, lhs, res)
    even, odd = dispatched(slots, entry_values(sums, order))
    half = low_half((tiles, LANES))
    pitch = out.shape[0] // tiles
    for i in range(SLOTS // 2):
        a, b = even[i * tiles : (i + 1) * tiles], odd[i * tiles : (i + 1) * tiles]
        out[pl.ds(i, tiles, stride=pitch), :] = jnp.where(half, a, b)


def solve_kernel(with_flux, p0, p1, p2, p3, *refs):
    rest = (p0, p1, p2, p3)
    if with_flux:
        mixing, extra, lev, out, buf, sems = refs
        groups = extra.shape[0]
        moves = [(rest, 0, 2 * groups, buf, 0)]
    else:
        *more, mixing, extra, lev, out, unit_out, buf, halo, sems = refs
        groups = extra.shape[0]
        moves = [
            (rest, 0, groups, buf, groups),
            (more[:4], 0, groups, buf, 0),
            (more[:4], groups, 8, buf, 2 * groups),
            (more[4:], 0, halo.shape[1], halo, 0),
        ]
    chunk = 16
    levels = 8
    copies = []
    for n, (parts, at, count, to, base) in enumerate(moves):
        for d, part in enumerate(parts):
            source = lax.rem(lev[0] + 4 - d, 4)
            copies.append(
                pltpu.make_async_copy(
                    part.at[pl.ds(at, count)], to.at[source, pl.ds(base, count)], sems.at[n, d]
                )
            )
    for copy in copies:
        copy.start()
    kbuf, ebuf = mixing.get(), extra.get()
    for copy in copies:
        copy.wait()
    if not with_flux:
        parts = [[[], []] for n in range(4)]
        for source in range(levels // 2):
            ends = [buf[source, 2 * groups + n : 2 * groups + n + 1, :] for n in range(4)]
            left, right = outer_rows(halo.at[source], lev[0] % 4, 0, lev)
            for n, rows in enumerate(((ends[0], ends[2]), (ends[1], ends[3]), left, right)):
                parts[n][0].append(rows[0])
                parts[n][1].append(rows[1])
        mended_rows = mended(*[[jnp.concatenate(rows, 0) for rows in part] for part in parts])
        for source in range(levels // 2):
            for n, row in enumerate((0, groups - 1)):
                old = buf[source, row : row + 1, :]
                new = mended_rows[n][source : source + 1]
                buf[source, row : row + 1, :] = mend(old, new, n == 1)

    def body(step, carry):
        at = pl.multiple_of(step * chunk, chunk)
        rows = pl.ds(at, chunk)
        k = [
            kbuf[pl.ds(at * levels + level, chunk, stride=levels), :] for level in range(levels)
        ]
        cs, ds, es = [], [], []
        for level in range(levels):
            r = buf[level // 2, pl.ds((level % 2) * groups + at, chunk), :]
            if level == 0:
                inverse = 1.0 / (1.0 + k[1])
                if with_flux:
                    r = r - ebuf[rows, :]
                else:
                    es.append(k[0] * ebuf[rows, :] * inverse)
                ds.append(r * inverse)
            else:
                total = 1.0 + k[level] - k[level] * cs[-1]
                if level + 1 < levels:
                    total = total + k[level + 1]
                inverse = 1.0 / total
                ds.append((r + k[level] * ds[-1]) * inverse)
                if not with_flux:
                    es.append(k[level] * es[-1] * inverse)
            if level + 1 < levels:
                cs.append(k[level + 1] * inverse)
        for terms, ref in ((ds, out),) if with_flux else ((ds, out), (es, unit_out)):
            x = terms[-1]
            ref[pl.ds(at * levels + levels - 1, chunk, stride=levels), :] = x
            for level in range(levels - 2, -1, -1):
                x = terms[level] + cs[level] * x
                ref[pl.ds(at * levels + level, chunk, stride=levels), :] = x
        return carry

    lax.fori_loop(0, groups // chunk, body, 0)


def last_kernel(arrived, labels, base, unit, out, gain, obuf, sems):
    tiles = labels.shape[0]
    groups = gain.shape[0]
    names = named_blocks(labels.get()[...], SLOTS, groups)
    (total,) = collected((slot_rows(arrived.get(), 0, SLOTS // 2, tiles),), names)
    gain[...] = total
    bbuf, ubuf = base.get(), unit.get()

    def body(step, carry):
        at = pl.ds(pl.multiple_of(step * 8, 8), 8)
        obuf[at, :] = bbuf[at, :] + ubuf[at, :] * gain[pl.ds(step, 1), :]
        return carry

    pieces = sems.shape[0]
    copies = []
    for n in range(pieces):
        lax.fori_loop(n * groups // pieces, (n + 1) * groups // pieces, body, 0, unroll=8)
        rows = pl.ds(n * 8 * groups // pieces, 8 * groups // pieces)
        copies.append(pltpu.make_async_copy(obuf.at[rows], out.at[rows], sems.at[n]))
        copies[n].start()
    for copy in copies:
        copy.wait()


VMEM = pl.BlockSpec(memory_space=pltpu.VMEM)
SMEM = pl.BlockSpec(memory_space=pltpu.SMEM)
HBM = pl.BlockSpec(memory_space=pltpu.HBM)
DMA = pltpu.SemaphoreType.DMA


def call(kernel, shapes, args, spaces, scratch=(), name=None, us=1.0, after=(), to=None):
    fetched = [i for i, space in enumerate(spaces) if space == "f"]
    outs = len(shapes) if isinstance(shapes, tuple) else 1

    def body(*refs):
        refs = list(refs)
        del refs[len(args) : len(args) + len(after)]
        end = len(refs) - 2 * len(fetched)
        for n, i in enumerate(fetched):
            refs[i] = Fetched(refs[i], refs[end + n], refs[end + len(fetched) + n])
        kernel(*refs[:end])

    extra = [pltpu.VMEM(args[i].shape, args[i].dtype) for i in fetched]
    extra += [DMA(()) for i in fetched]
    return pl.pallas_call(
        body,
        out_shape=shapes,
        in_specs=[{"v": VMEM, "s": SMEM, "h": HBM, "f": HBM}[space] for space in spaces]
        + [HBM] * len(after),
        out_specs=jax.tree.map(lambda _: VMEM, shapes) if to is None else to,
        scratch_shapes=list(scratch) + extra,
        compiler_params=pltpu.CompilerParams(vmem_limit_bytes=64 * 1024 * 1024),
        cost_estimate=pl.CostEstimate(
            flops=0, bytes_accessed=int(us * 3.6e6), transcendentals=0
        ),
        name=name,
    )(*args, *after)


def shape(*dims, dtype=F32):
    return jax.ShapeDtypeStruct(dims, dtype)


def tile_rows(x, lead):
    levels, cells = x.shape[-2:]
    x = x.reshape(lead, levels, cells // LANES, LANES)
    return x.transpose(0, 2, 1, 3).reshape(lead * levels * cells // LANES, LANES)


def weight_rows(w):
    blocks, fan, size = w.shape
    w = w.reshape(blocks, fan, size // LANES, LANES).transpose(0, 2, 1, 3)
    return w.reshape(blocks * fan * size // LANES, LANES)


def on_device(
    air_state,
    sea_state,
    air_courant,
    sea_courant,
    air_mixing,
    sea_mixing,
    upward_weight,
    upward_target,
    upward_block,
    downward_weight,
    downward_target,
    downward_block,
    sea_mask,
):
    fields, pair, cells = air_state.shape
    tiles = lax.axis_size("tiles")
    levs = lax.axis_size("lev")
    rows = cells // LANES
    groups = sea_mask.shape[0] // 2
    lev = lax.axis_index("lev").astype(jnp.int32)
    tile = lax.axis_index("tiles").astype(jnp.int32)
    lev_ref = (lev + levs * (tile % 2)).reshape(1)
    states = (
        tile_rows(sea_state, fields),
        tile_rows(air_state, fields),
        tile_rows(sea_courant, 1),
        tile_rows(air_courant, 1),
    )
    size = pair * rows

    to_pair, to_other = call(
        edge_kernel,
        (shape(20, LANES),) * 2,
        (*states, lev_ref),
        "hhhhs",
        scratch=[
            pltpu.VMEM((2, fields + 1, 8, LANES), F32),
            pltpu.VMEM((2, fields + 1, 8, LANES), F32),
            DMA((2, fields + 1, 2)),
        ],
        name="edges",
        us=1.5,
    )
    pairs = [(i, i + 1 - 2 * (i % 2)) for i in range(tiles)]
    others = [(i, (i - 1 + 2 * (i % 2)) % tiles) for i in range(tiles)]
    from_other = lax.ppermute(to_other, "tiles", others)
    ends = (lax.ppermute(to_pair, "tiles", pairs), from_other)
    extended = pltpu.VMEM((rows + 16, LANES), F32)

    def around(parts):
        return [parts[0]] + [
            lax.ppermute(parts[d], "lev", [(i, (i + d) % levs) for i in range(levs)])
            for d in range(1, levs)
        ]

    sea_own = call(
        functools.partial(sea_kernel, fields),
        (shape(rows + 8, LANES),) * 4,
        (states[0], states[2], lev_ref),
        "hfs",
        scratch=[pltpu.VMEM((4, size, LANES), F32), DMA((4,))],
        name="sea",
        us=3.0,
        after=(to_pair,),
    )
    sea = around(sea_own)
    entries = 4 * groups
    place_up, place_down, labels, mask, ready = call(
        functools.partial(prepare_kernel, tiles),
        (
            shape(2, entries, dtype=jnp.int32),
            shape(2, entries, dtype=jnp.int32),
            shape(tiles, LANES),
            shape(groups, LANES),
            shape(8, LANES),
        ),
        (
            upward_target.T,
            upward_block.T,
            downward_target.T,
            downward_block.T,
            sea_mask.reshape(1, -1),
        ),
        "fffff",
        name="prepare",
        us=2.5,
        after=(sea_own[0],),
    )
    halo = around([jnp.concatenate([*ends, ready], 0)] * 4)
    air_k = tile_rows(air_mixing, 1)
    sea_k = tile_rows(sea_mixing, 1)
    up_rows = weight_rows(upward_weight)
    down_rows = weight_rows(downward_weight)

    def workspace(count):
        return [
            pltpu.VMEM(up_rows.shape, BF16),
            pltpu.VMEM((groups * count, LANES), F32),
            pltpu.VMEM((groups * count, LANES), F32),
        ]

    pitch = SLOTS + 1
    outgoing = call(
        up_kernel,
        shape(tiles * pitch, LANES),
        (*sea, *halo, mask, place_up, labels, up_rows, lev_ref),
        "hhhhhhhhfffhs",
        scratch=[
            pltpu.VMEM((rows + 8, LANES), F32),
            pltpu.VMEM(halo[0].shape, F32),
            *workspace(16),
            DMA((2,)),
            DMA((PIECES,)),
        ],
        name="upward",
        us=8.0,
    )

    def over_tiles(x):
        pitch = x.shape[0] // tiles
        y = x.reshape((tiles, pitch, LANES) if pitch % 8 == 0 else (tiles, 1, pitch * LANES))
        y = lax.all_to_all(y, "tiles", split_axis=0, concat_axis=0, tiled=True)
        return y.reshape(x.shape)

    *rest, factor = call(
        functools.partial(advect_kernel, fields),
        (shape(size, LANES),) * 4 + (shape(rows, LANES),) * 5,
        (*states, air_k, *ends, lev_ref),
        "fffffffs",
        scratch=[pltpu.VMEM((20, LANES), F32)] * 2 + [extended, extended],
        name="advect",
        us=4.0,
        after=(outgoing,),
    )
    air = around(rest[:4])
    arrived = over_tiles(outgoing)
    flux, returning, labels_down = call(
        middle_kernel,
        (shape(groups, LANES), shape(tiles * SLOTS // 2, LANES), shape(tiles, LANES)),
        (arrived, *air, factor, place_down, down_rows, lev_ref),
        "fhhhhffhs",
        scratch=[pltpu.VMEM((rows, LANES), F32), *workspace(8), DMA(()), DMA((PIECES,))],
        name="middle",
        us=8.0,
    )
    gained = over_tiles(returning)
    sea_rest = around(rest[4:])

    column = shape(8 * rows, LANES)

    def solve(with_flux, parts, k, extra, name, after=()):
        buf = pltpu.VMEM((4, 2 * rows if with_flux else 2 * rows + 8, LANES), F32)
        return call(
            functools.partial(solve_kernel, with_flux),
            column if with_flux else (column, column),
            (*parts, k, extra, lev_ref),
            "h" * len(parts) + "ffs",
            scratch=[
                buf,
                *([] if with_flux else [pltpu.VMEM((4, *halo[0].shape), F32)]),
                DMA((1 if with_flux else 4, 4)),
            ],
            name=name,
            us=3.0,
            after=after,
        )

    air_out = solve(True, air, air_k, flux, "solve_air")
    base, unit = solve(False, [*sea_rest, *sea, *halo], sea_k, mask, "solve_sea", (air_out,))
    sea_out = call(
        last_kernel,
        column,
        (gained, labels_down, base, unit),
        "ffff",
        scratch=[pltpu.VMEM((rows, LANES), F32), pltpu.VMEM((8 * rows, LANES), F32), DMA((4,))],
        name="last",
        to=HBM,
        us=2.0,
    )

    def levels_first(x):
        return x.reshape(rows, 8, LANES).transpose(1, 0, 2).reshape(1, 8, cells)

    return levels_first(air_out), levels_first(sea_out)


def solution(mesh):
    return jax.shard_map(
        on_device,
        mesh=mesh,
        in_specs=(
            P(None, "lev", "tiles"),
            P(None, "lev", "tiles"),
            P("lev", "tiles"),
            P("lev", "tiles"),
            P(None, "tiles"),
            P(None, "tiles"),
            P("tiles", None, None),
            P("tiles", None),
            P("tiles", None),
            P("tiles", None, None),
            P("tiles", None),
            P("tiles", None),
            P("tiles"),
        ),
        out_specs=(P("lev", None, "tiles"), P("lev", None, "tiles")),
        check_vma=False,
    )
```
